256 devices in a mesh: param: 64 (over z, x, core), tok: 2 (over y_lo), probe: 2 (over y_hi).
Axes of the slice: x: 4, y: 4 (y_hi: 2, y_lo: 2; y = y_hi * 2 + y_lo), z: 8, core: 2. Of those that a mesh axis runs over, the one named last changes fastest.
Arguments:
- tokens_x: bfloat16 [1024, 8192], P('tok'), may hold values from -6 to 6
- cotangent: bfloat16 [2, 1024, 14336], P('probe', 'tok', 'param'), may hold values from -6 to 6
- signs: int32 [134217728], P(('param', 'tok')), may hold values from -1 to 1, as said below
- samples: int32 [16384], replicated, may hold values from 0 to 134217727
Outputs:
- sketch: float32 [2, 16384], P(None, 'probe')
- basis: float32 [2, 16384], P(None, 'probe')
The draws below stay inside these ranges and needn't reach their ends.
Inputs may be any that keep to these rules, and one draw needn't show every extreme that they name: `signs`: every entry is +1 or -1.
All inputs are finite; a program needn't handle non-finite values.
Results may differ from the reference program's by a relative error of at most 0.0003.
Values sent between devices are 32-bit elements; how exact they have to be, the bound alone decides.
A program may use at most 128 MiB of HBM per device.

```python
import jax
import jax.numpy as jnp
from jax import lax

D = 8192
FFH = 14336
LENGTH = 134217728
SAMPLES = 16384
TOKENS = 1024
PROBES = 2
COLS = 224
PADCOL = 256
N_PARAM = 64


def draw_signs(key, part):
    key = jax.random.fold_in(key, 11)
    coins = jax.random.randint(key, (LENGTH,), 0, 2)
    return (2 * coins - 1).astype(jnp.int32)


def plant(drawn, key, least, largest):
    shape = drawn.shape
    place = [jax.random.randint(jax.random.fold_in(key, axis), (), 0, shape[axis]) for axis in range(len(shape))]
    drawn = drawn.at[tuple(place)].set(least)
    longest = shape.index(max(shape))
    place[longest] = (place[longest] + 1) % shape[longest]
    return drawn.at[tuple(place)].set(largest)


def steps_of(own_key, shape, cuts, low, high):
    loudness = 1.0
    for dim, shards_of in cuts:
        steps = jax.random.uniform(jax.random.fold_in(jax.random.fold_in(own_key, 6), dim), (shards_of,), jnp.float32, low / len(cuts), high / len(cuts))
        loudness = loudness * jnp.repeat(jnp.exp(steps), shape[dim] // shards_of).reshape((-1,) + (1,) * (len(shape) - 1 - dim))
    return loudness


def scatter_about(stream_key, dims, scale, limit, split=(), kind=jnp.bfloat16):
    result = scale * jax.random.normal(stream_key, dims, jnp.float32)
    if split:
        result = result * steps_of(stream_key, dims, split, -0.22, 0.18)
    return jnp.clip(result, -limit, limit).astype(kind)


def setup_inputs(seed: int = 0) -> dict:
    seeds = jax.random.split(jax.random.key(seed), 5)
    return {
        "tokens_x": scatter_about(seeds[0], (TOKENS, D), 1.0, 6.0, ((0, 2),)),
        "cotangent": scatter_about(seeds[1], (PROBES, TOKENS, FFH), 1.0, 6.0, ((0, 2), (1, 2), (2, 64))),
        "signs": draw_signs(jax.random.fold_in(seeds[4], 71), 0),
        "samples": plant(jax.random.randint(seeds[3], (SAMPLES,), 0, LENGTH), jax.random.fold_in(seeds[3], 1), 0, LENGTH - 1).astype(jnp.int32),
    }


def bit_parity(value, bits):
    total = jnp.zeros_like(value)
    for shift_bit in range(bits):
        total = total + (value >> shift_bit & 1)
    return total & 1

def hadamard_table(width):
    index = jnp.arange(width, dtype=jnp.int32)
    parity = bit_parity(index[:, None] & index[None, :], width.bit_length())
    return (1 - 2 * parity).astype(jnp.float32)

def hadamard(vector):
    length = vector.shape[0]
    total_bits = length.bit_length() - 1
    done = 0
    while done < total_bits:
        step_bits = min(7, total_bits - done)
        width = 2 ** step_bits
        table = hadamard_table(width)
        if done == 0:
            vector = jnp.dot(vector.reshape(-1, width), table, precision=lax.Precision.HIGHEST)
        else:
            shaped = vector.reshape(length // 2 ** (done + step_bits), width, 2 ** done)
            vector = jnp.einsum('fg,agb->afb', table, shaped, precision=lax.Precision.HIGHEST)
        vector = vector.reshape(length)
        done = done + step_bits
    return vector

def reference(tokens_x, cotangent, signs, samples):
    scale = float(TOKENS * LENGTH) ** (-0.5)
    signed_float = signs.astype(jnp.float32)
    rows = []
    for probe_id in range(PROBES):
        grad = jnp.dot(tokens_x.T, cotangent[probe_id], preferred_element_type=jnp.float32)
        blocks = grad.reshape(D, N_PARAM, COLS).transpose(1, 0, 2)
        blocks = jnp.pad(blocks, ((0, 0), (0, 0), (0, PADCOL - COLS)))
        vector = blocks.reshape(LENGTH) * signed_float
        mixed = hadamard(vector)
        rows.append(jnp.take(mixed, samples) * scale)
    sketch = jnp.stack(rows)
    first = sketch[0]
    unit = first * lax.rsqrt(jnp.mean(first * first) + 1e-06)
    proj = jnp.mean(unit * sketch[1])
    rest = sketch[1] - proj * unit
    second = rest * lax.rsqrt(jnp.mean(rest * rest) + 1e-06)
    basis = jnp.stack([unit, second])
    return (sketch, basis)
```

```python
import functools

import jax
import jax.numpy as jnp
from jax import lax
from jax.experimental import pallas as pl
from jax.experimental.pallas import tpu as pltpu
from jax.sharding import PartitionSpec as P

MESH = pl.DeviceIdType.MESH
RING_X, RING_Z = 4, 8
SIDE = 256
BF16, F32 = jnp.bfloat16, jnp.float32


def position():
    param = lax.axis_index("param")
    z, x, core = param // 8, (param // 2) % 4, param % 2
    return z, x, core, lax.axis_index("tok"), lax.axis_index("probe")


def device(z, x, core, tok, probe):
    return ((z * RING_X + x) * 2 + core, tok, probe)


def wrap(value, size):
    return lax.rem(value + 2 * size, size)


def signed_table(width):
    rows = lax.broadcasted_iota(jnp.int32, (width, width), 0)
    cols = lax.broadcasted_iota(jnp.int32, (width, width), 1)
    bits = rows & cols
    bits = bits ^ (bits >> 4)
    bits = bits ^ (bits >> 2)
    bits = bits ^ (bits >> 1)
    return (1 - 2 * (bits & 1)).astype(F32).astype(BF16)


def split_two(value):
    high = value.astype(BF16)
    return high, (value - high.astype(F32)).astype(BF16)


def butterfly(values):
    values = list(values)
    gap = 1
    while gap < len(values):
        for start in range(0, len(values), 2 * gap):
            for i in range(start, start + gap):
                a, b = values[i], values[i + gap]
                values[i], values[i + gap] = a + b, a - b
        gap *= 2
    return values


def transform_kernel(
    x_ref, ct_ref, signs_ref, out_ref,
    xh, xfb, zfb, xf, zf, sg, ct_raw, ct_send, ct_land, ct_own, ct_other, table,
    xo, base, sign_t, f_own, f_sib, local_sem, send_sem, recv_sem,
):
    z, x, core, tok, probe = position()
    half = 4096
    near = device(z, x, core, 1 - tok, probe)
    far = device(z, x, core, 1 - tok, 1 - probe)
    right_x = device(z, wrap(x + 1, RING_X), core, tok, probe)
    left_x = device(z, wrap(x - 1, RING_X), core, tok, probe)
    right_z = device(wrap(z + 1, RING_Z), x, core, tok, probe)
    left_z = device(wrap(z - 1, RING_Z), x, core, tok, probe)
    sibling = device(z, x, 1 - core, tok, probe)

    mine = pl.multiple_of(tok * half, 128)
    theirs = pl.multiple_of((1 - tok) * half + core * 2048, 128)
    loads = [
        pltpu.make_async_copy(ct_ref, ct_raw, local_sem.at[0]),
        pltpu.make_async_copy(
            x_ref.at[pl.ds(pl.multiple_of(64 * z, 64), 64), pl.ds(theirs + 1024, 1024)], zfb, local_sem.at[1]),
        pltpu.make_async_copy(
            x_ref.at[pl.ds(pl.multiple_of(128 * x, 128), 128), pl.ds(theirs, 1024)], xfb, local_sem.at[2]),
        pltpu.make_async_copy(x_ref.at[:, pl.ds(mine, half)], xh, local_sem.at[3]),
        pltpu.make_async_copy(signs_ref, sg, local_sem.at[4]),
    ]
    for load in loads:
        load.start()

    barrier = pltpu.get_barrier_semaphore()
    for other in (near, far, right_x, left_x, right_z, left_z, sibling):
        pl.semaphore_signal(barrier, inc=1, device_id=other, device_id_type=MESH)

    numbers = {}
    sent = []

    def number(name):
        return numbers.setdefault(name, len(numbers))

    def send(name, src, dst, target):
        n = number(name)
        copy = pltpu.make_async_remote_copy(
            src_ref=src, dst_ref=dst, send_sem=send_sem.at[n], recv_sem=recv_sem.at[n],
            device_id=target, device_id_type=MESH)
        copy.start()
        sent.append(copy)

    def arrived(name, dst, source):
        n = number(name)
        pltpu.make_async_remote_copy(
            src_ref=dst, dst_ref=dst, send_sem=send_sem.at[n], recv_sem=recv_sem.at[n],
            device_id=source, device_id_type=MESH).wait_recv()

    def xs(j, i):
        return xo.at[core * 8 + j, pl.ds(pl.multiple_of(128 * wrap(i, RING_X), 128), 128)]

    def zs(j, i):
        return xo.at[core * 8 + 4 + j, pl.ds(pl.multiple_of(64 * wrap(i, RING_Z), 64), 64)]

    loads[0].wait()
    ct_send[...] = ct_raw[...].astype(F32)
    loads[1].wait()
    for j in range(4):
        zf[j] = zfb[:, j * SIDE:(j + 1) * SIDE].astype(F32)
    loads[2].wait()
    for j in range(4):
        xf[j] = xfb[:, j * SIDE:(j + 1) * SIDE].astype(F32)
    pl.semaphore_wait(barrier, 7)

    send("ct", ct_send, ct_land, near)
    route = [far, far, far, near]
    for j in range(4):
        send(("zy", j), zf.at[j], zs(j, z), route[j])
        send(("xy", j), xf.at[j], xs(j, x), route[j])

    table[...] = signed_table(SIDE)
    ct_own[...] = jnp.zeros_like(ct_own)
    ct_other[...] = jnp.zeros_like(ct_other)
    ct_own[0:224, :] = ct_raw[...]
    loads[3].wait()
    loads[4].wait()

    def prepare(first):
        def body(i, carry):
            g = first + i
            even = sg[pl.ds(pl.multiple_of(512 * g, 512), SIDE, stride=2), :]
            odd = sg[pl.ds(pl.multiple_of(512 * g, 512) + 1, SIDE, stride=2), :]
            turned = jnp.concatenate([even.astype(F32).T, odd.astype(F32).T], axis=0)
            product = jnp.dot(
                ct_own[...], xh[:, pl.ds(pl.multiple_of(SIDE * g, SIDE), SIDE)], preferred_element_type=F32)
            sign_t[g] = turned
            base[g] = turned * product
            return carry

        lax.fori_loop(0, 4, body, 0)

    def process(g):
        h = table[...]
        product = jnp.dot(ct_other[...], xo[g].astype(BF16), preferred_element_type=F32)
        high, low = split_two(base[g] + sign_t[g] * product)
        mixed = jnp.dot(h, high, preferred_element_type=F32) + jnp.dot(h, low, preferred_element_type=F32)
        high, low = split_two(mixed)
        mixed = jnp.dot(high, h, preferred_element_type=F32) + jnp.dot(low, h, preferred_element_type=F32)
        f_own[2 * g] = mixed[:, 0:128]
        f_own[2 * g + 1] = mixed[:, 128:256]

    def process_mine(k):
        g = core * 8 + k
        process(g)
        send(("f0", k), f_own.at[pl.ds(2 * g, 2)], f_sib.at[pl.ds(2 * g, 2)], sibling)

    def process_theirs(k):
        g = (1 - core) * 8 + k
        arrived(("share", k), xo.at[g], sibling)
        process(g)
        send(("f1", k), f_own.at[pl.ds(2 * g, 2)], f_sib.at[pl.ds(2 * g, 2)], sibling)

    def take_ct():
        arrived("ct", ct_land, near)
        ct_other[0:224, :] = ct_land[...].astype(BF16)

    def complete(k):
        g = core * 8 + k
        send(("share", k), xo.at[g], xo.at[g], sibling)

    def x0(j):
        arrived(("xy", j), xs(j, x), route[j])
        send(("xr", j), xs(j, x), xs(j, x), right_x)
        send(("xl", j), xs(j, x), xs(j, x), left_x)

    def x1(j):
        arrived(("xr", j), xs(j, x - 1), left_x)
        if j % 2 == 0:
            send(("xe", j), xs(j, x - 1), xs(j, x - 1), right_x)
        arrived(("xl", j), xs(j, x + 1), right_x)
        if j % 2 == 1:
            send(("xe", j), xs(j, x + 1), xs(j, x + 1), left_x)

    def x2(j):
        arrived(("xe", j), xs(j, x + 2), left_x if j % 2 == 0 else right_x)
        complete(j)

    def z0(j):
        arrived(("zy", j), zs(j, z), route[j])
        send(("zr", j, 1), zs(j, z), zs(j, z), right_z)
        send(("zl", j, 1), zs(j, z), zs(j, z), left_z)

    def zh(j, d):
        arrived(("zr", j, d), zs(j, z - d), left_z)
        if d < 3 or j % 2 == 0:
            send(("zr", j, d + 1), zs(j, z - d), zs(j, z - d), right_z)
        arrived(("zl", j, d), zs(j, z + d), right_z)
        if d < 3 or j % 2 == 1:
            send(("zl", j, d + 1), zs(j, z + d), zs(j, z + d), left_z)

    def z4(j):
        if j % 2 == 0:
            arrived(("zr", j, 4), zs(j, z - 4), left_z)
        else:
            arrived(("zl", j, 4), zs(j, z + 4), right_z)
        complete(4 + j)

    steps = [(0.5 + 1.5 * i, functools.partial(prepare, 4 * i)) for i in range(4)]
    steps.append((9.9, take_ct))
    for j in range(4):
        at = 4.2 + 4.2 * j
        done = at + 4.2
        steps += [(at, functools.partial(x0, j)), (at + 2.5, functools.partial(x1, j)), (done, functools.partial(x2, j))]
        steps += [(max(done, 10.0) + 0.1, functools.partial(process_mine, j)),
                  (max(done, 10.0) + 1.5, functools.partial(process_theirs, j))]
        at = 1.4 + 4.9 * j
        done = at + 6.4
        steps.append((at, functools.partial(z0, j)))
        steps += [(at + 1.6 * d, functools.partial(zh, j, d)) for d in (1, 2, 3)]
        steps.append((done, functools.partial(z4, j)))
        steps += [(max(done, 10.0) + 0.1, functools.partial(process_mine, 4 + j)),
                  (max(done, 10.0) + 1.5, functools.partial(process_theirs, 4 + j))]
    for _, step in sorted(steps, key=lambda entry: entry[0]):
        step()

    for k in range(8):
        g = (1 - core) * 8 + k
        arrived(("f0", k), f_sib.at[pl.ds(2 * g, 2)], sibling)
        g = core * 8 + k
        arrived(("f1", k), f_sib.at[pl.ds(2 * g, 2)], sibling)

    flip = (1 - 2 * core).astype(F32)

    def last(i, carry):
        part, row = i // 32, pl.multiple_of((i % 32) * 8, 8)
        own = [f_own[2 * g + part, pl.ds(row, 8), :] for g in range(16)]
        sib = [f_sib[2 * g + part, pl.ds(row, 8), :] for g in range(16)]
        plus = butterfly([a + b for a, b in zip(own, sib)])
        minus = butterfly([(a - b) * flip for a, b in zip(own, sib)])
        for g in range(16):
            out_ref[0, 2 * g + part, pl.ds(row, 8), :] = plus[g]
            out_ref[1, 2 * g + part, pl.ds(row, 8), :] = minus[g]
        return carry

    lax.fori_loop(0, 64, last, 0)
    for copy in sent:
        copy.wait_send()


def transform(tokens_x, cot_t, signs):
    copies = 96
    return pl.pallas_call(
        transform_kernel,
        out_shape=jax.ShapeDtypeStruct((2, 32, SIDE, 128), F32),
        in_specs=[pl.BlockSpec(memory_space=pl.ANY)] * 3,
        out_specs=pl.BlockSpec(memory_space=pltpu.VMEM),
        scratch_shapes=[
            pltpu.VMEM((512, 4096), BF16),
            pltpu.VMEM((128, 1024), BF16),
            pltpu.VMEM((64, 1024), BF16),
            pltpu.VMEM((4, 128, SIDE), F32),
            pltpu.VMEM((4, 64, SIDE), F32),
            pltpu.VMEM((8192, 128), jnp.int32),
            pltpu.VMEM((224, 512), BF16),
            pltpu.VMEM((224, 512), F32),
            pltpu.VMEM((224, 512), F32),
            pltpu.VMEM((SIDE, 512), BF16),
            pltpu.VMEM((SIDE, 512), BF16),
            pltpu.VMEM((SIDE, SIDE), BF16),
            pltpu.VMEM((16, 512, SIDE), F32),
            pltpu.VMEM((16, SIDE, SIDE), F32),
            pltpu.VMEM((16, SIDE, SIDE), F32),
            pltpu.VMEM((32, SIDE, 128), F32),
            pltpu.VMEM((32, SIDE, 128), F32),
            pltpu.SemaphoreType.DMA((5,)),
            pltpu.SemaphoreType.DMA((copies,)),
            pltpu.SemaphoreType.DMA((copies,)),
        ],
        compiler_params=pltpu.CompilerParams(
            collective_id=0, has_side_effects=True, vmem_limit_bytes=50 << 20),
        cost_estimate=pl.CostEstimate(flops=8 << 30, bytes_accessed=24 << 20, transcendentals=0),
        name="transform",
    )(tokens_x, cot_t, signs)


def sketch_kernel(
    index_ref, samples_ref, t_ref, sketch_ref, basis_ref,
    rows, mine, land_xt, red, land_z, full, send_sem, recv_sem,
):
    z, x, core, tok, probe = position()
    lane_mates = [((i // 2), i % 2) for i in range(1, 8)]
    me = x * 2 + tok

    def xt_device(member):
        return device(z, member // 2, core, member % 2, probe)

    group = [(dx, dt, dp, dc) for dx in range(4) for dt in range(2) for dp in range(2) for dc in range(2)][1:]

    def group_device(offset):
        dx, dt, dp, dc = offset
        return device(z, wrap(x + dx, RING_X), core ^ dc, tok ^ dt, probe ^ dp)

    def group_source(offset):
        dx, dt, dp, dc = offset
        return wrap(x - dx, RING_X), core ^ dc, tok ^ dt, probe ^ dp

    barrier = pltpu.get_barrier_semaphore()
    for offset in group:
        pl.semaphore_signal(barrier, inc=1, device_id=group_device(offset), device_id_type=MESH)
    for d in range(1, 8):
        pl.semaphore_signal(
            barrier, inc=1, device_id=device(wrap(z + d, RING_Z), x, core, tok, probe), device_id_type=MESH)

    code = tok | (x << 2) | (z << 4)
    lanes = lax.broadcasted_iota(jnp.int32, (128, 128), 0)

    def gather_piece(piece):
        row0 = core * 64 + piece * 8

        def body(b, carry):
            row = row0 + b
            for k in range(128):
                rows[k:k + 1, :] = t_ref[pl.ds(index_ref[row * 128 + k], 1), :]
            m = samples_ref[pl.ds(row, 1), :]
            picked = jnp.where(lanes == ((m >> 8) & 127), rows[...].T, 0.0)
            value = jnp.sum(picked, axis=0, keepdims=True)
            odd = (m >> 20) & code
            odd = odd ^ (odd >> 4)
            odd = odd ^ (odd >> 2)
            odd = odd ^ (odd >> 1)
            mine[piece, pl.ds(b, 1), :] = jnp.where((odd & 1) == 1, -value, value)
            return carry

        lax.fori_loop(0, 8, body, 0)

    sent = []
    for d in range(1, 8):
        piece = wrap(me + d, 8)
        gather_piece(piece)
        if d == 1:
            pl.semaphore_wait(barrier, 38)
        copy = pltpu.make_async_remote_copy(
            src_ref=mine.at[piece], dst_ref=land_xt.at[d - 1], send_sem=send_sem.at[d - 1],
            recv_sem=recv_sem.at[d - 1], device_id=xt_device(piece), device_id_type=MESH)
        copy.start()
        sent.append(copy)
    gather_piece(me)
    total = mine[me]
    for d in range(1, 8):
        pltpu.make_async_remote_copy(
            src_ref=land_xt.at[d - 1], dst_ref=land_xt.at[d - 1], send_sem=send_sem.at[d - 1],
            recv_sem=recv_sem.at[d - 1], device_id=xt_device(wrap(me - d, 8)), device_id_type=MESH).wait_recv()
        total = total + land_xt[d - 1]
    red[...] = total

    def z_copy(source, target):
        return pltpu.make_async_remote_copy(
            src_ref=red, dst_ref=land_z.at[source], send_sem=send_sem.at[7 + target],
            recv_sem=recv_sem.at[7 + source], device_id=device(target, x, core, tok, probe), device_id_type=MESH)

    for d in range(1, 8):
        copy = z_copy(z, wrap(z + d, RING_Z))
        copy.start()
        sent.append(copy)
    land_z[z] = total
    for d in range(1, 8):
        z_copy(wrap(z - d, RING_Z), z).wait_recv()
    total = land_z[0]
    for i in range(1, 8):
        total = total + land_z[i]
    scale = float(1024 * 134217728) ** (-0.5)

    def place(px, pcore, ptok, pprobe):
        return full.at[pprobe, pl.ds(pl.multiple_of(pcore * 64 + (px * 2 + ptok) * 8, 8), 8)]

    here = place(x, core, tok, probe)
    here[...] = total * scale
    for i, offset in enumerate(group):
        copy = pltpu.make_async_remote_copy(
            src_ref=here, dst_ref=here, send_sem=send_sem.at[15 + i], recv_sem=recv_sem.at[15 + i],
            device_id=group_device(offset), device_id_type=MESH)
        copy.start()
        sent.append(copy)
    for i, offset in enumerate(group):
        px, pcore, ptok, pprobe = group_source(offset)
        there = place(px, pcore, ptok, pprobe)
        pltpu.make_async_remote_copy(
            src_ref=there, dst_ref=there, send_sem=send_sem.at[15 + i], recv_sem=recv_sem.at[15 + i],
            device_id=device(z, px, pcore, ptok, pprobe), device_id_type=MESH).wait_recv()

    count = 16384.0

    def mean(value):
        return jnp.sum(jnp.sum(value, axis=0, keepdims=True), axis=1, keepdims=True) / count

    first, second = full[0], full[1]
    unit = first * lax.rsqrt(mean(first * first) + 1e-06)
    rest = second - mean(unit * second) * unit
    last = rest * lax.rsqrt(mean(rest * rest) + 1e-06)
    rows[...] = unit
    land_rest = land_z
    start = pl.multiple_of(probe * 64, 64)
    for i in range(64):
        cols = slice(i * 128, (i + 1) * 128)
        sketch_ref[0:1, cols] = full[0, pl.ds(start + i, 1), :]
        sketch_ref[1:2, cols] = full[1, pl.ds(start + i, 1), :]
        basis_ref[0:1, cols] = rows[pl.ds(start + i, 1), :]
    rows[...] = last
    for i in range(64):
        basis_ref[1:2, i * 128:(i + 1) * 128] = rows[pl.ds(start + i, 1), :]
    for copy in sent:
        copy.wait_send()


def sketch(samples, table):
    index = ((samples >> 21 & 1) << 13) | ((samples >> 15 & 31) << 8) | (samples & 255)
    shape = jax.ShapeDtypeStruct((2, 8192), F32)
    return pl.pallas_call(
        sketch_kernel,
        out_shape=(shape, shape),
        in_specs=[
            pl.BlockSpec(memory_space=pltpu.SMEM),
            pl.BlockSpec(memory_space=pltpu.VMEM),
            pl.BlockSpec(memory_space=pltpu.VMEM),
        ],
        out_specs=(pl.BlockSpec(memory_space=pltpu.VMEM), pl.BlockSpec(memory_space=pltpu.VMEM)),
        scratch_shapes=[
            pltpu.VMEM((128, 128), F32),
            pltpu.VMEM((8, 8, 128), F32),
            pltpu.VMEM((7, 8, 128), F32),
            pltpu.VMEM((8, 128), F32),
            pltpu.VMEM((8, 8, 128), F32),
            pltpu.VMEM((2, 128, 128), F32),
            pltpu.SemaphoreType.DMA((46,)),
            pltpu.SemaphoreType.DMA((46,)),
        ],
        compiler_params=pltpu.CompilerParams(
            collective_id=1, has_side_effects=True, vmem_limit_bytes=24 << 20),
        cost_estimate=pl.CostEstimate(flops=1 << 24, bytes_accessed=8 << 20, transcendentals=0),
        name="sketch",
    )(index, samples.reshape(128, 128), table)


def on_device(tokens_x, cotangent, signs, samples):
    table = transform(tokens_x, cotangent[0].T, signs.reshape(8192, 128))
    return sketch(samples, table.reshape(16384, 128))


def solution(mesh):
    in_specs = (P("tok", None), P("probe", "tok", "param"), P(("param", "tok")), P())
    out_specs = (P(None, "probe"), P(None, "probe"))
    return jax.shard_map(
        on_device, mesh=mesh, in_specs=in_specs, out_specs=out_specs, check_vma=False
    )
```

```python
import functools

import jax
import jax.numpy as jnp
from jax import lax
from jax.experimental import pallas as pl
from jax.experimental.pallas import tpu as pltpu
from jax.sharding import PartitionSpec as P

MESH = pl.DeviceIdType.MESH
RING_X, RING_Z = 4, 8
SIDE = 256
BF16, F32 = jnp.bfloat16, jnp.float32


def position():
    param = lax.axis_index("param")
    z, x, core = param // 8, (param // 2) % 4, param % 2
    return z, x, core, lax.axis_index("tok"), lax.axis_index("probe")


def device(z, x, core, tok, probe):
    return ((z * RING_X + x) * 2 + core, tok, probe)


def wrap(value, size):
    return lax.rem(value + 2 * size, size)


def signed_table(width):
    rows = lax.broadcasted_iota(jnp.int32, (width, width), 0)
    cols = lax.broadcasted_iota(jnp.int32, (width, width), 1)
    bits = rows & cols
    bits = bits ^ (bits >> 4)
    bits = bits ^ (bits >> 2)
    bits = bits ^ (bits >> 1)
    return (1 - 2 * (bits & 1)).astype(F32).astype(BF16)


def split_two(value):
    high = value.astype(BF16)
    return high, (value - high.astype(F32)).astype(BF16)


def butterfly(values):
    values = list(values)
    gap = 1
    while gap < len(values):
        for start in range(0, len(values), 2 * gap):
            for i in range(start, start + gap):
                a, b = values[i], values[i + gap]
                values[i], values[i + gap] = a + b, a - b
        gap *= 2
    return values


FEED = (("f", 5), ("n", 2), ("f", 4), ("n", 3), ("f", 6), ("n", "ct"), ("f", 0), ("n", 7), ("f", 1), ("f", 7))
ORDER = (
    "p00 p10 p20 p30", "z50 z40 x20 z60", "z51 x30 z41 x00", "z61 x21 z52 x10", "z42 x31 z62 z53",
    "x01 z43 c00 z63", "x22 m20 z54 m50", "z44 m40 t20 x32", "x11 m30 z64 t50", "m60 t40 y70 t30",
    "x02 m70 m00 t60", "q20 x12 t70 m10", "t00 q10 t10 q30", "q00",
)


def whole_kernel(
    x_ref, ct_ref, signs_ref, samples_ref, sketch_ref, basis_ref,
    xh, xfb, zfb, yfb, xf, zf, yf, sg, ct_raw, ct_send, ct_land, ct_own, ct_other, table,
    xo, base, sign_t, f_own, f_sib, grid, samples, index_v, index_s,
    rows, mine, land_xt, red, land_z, full,
    local_sem, send_sem, recv_sem, send_small, recv_small,
):
    z, x, core, tok, probe = position()
    half = 4096
    near = device(z, x, core, 1 - tok, probe)
    far = device(z, x, core, 1 - tok, 1 - probe)
    right_x = device(z, wrap(x + 1, RING_X), core, tok, probe)
    left_x = device(z, wrap(x - 1, RING_X), core, tok, probe)
    right_z = device(wrap(z + 1, RING_Z), x, core, tok, probe)
    left_z = device(wrap(z - 1, RING_Z), x, core, tok, probe)
    sibling = device(z, x, 1 - core, tok, probe)
    group = [(dx, dt, dp, dc) for dx in range(4) for dt in range(2) for dp in range(2) for dc in range(2)][1:]

    def group_device(offset):
        dx, dt, dp, dc = offset
        return device(z, wrap(x + dx, RING_X), core ^ dc, tok ^ dt, probe ^ dp)

    mine_at = pl.multiple_of(tok * half, 128)
    theirs = pl.multiple_of((1 - tok) * half + core * 2048, 128)
    loads = [
        pltpu.make_async_copy(
            x_ref.at[pl.ds(pl.multiple_of(64 * z, 64), 64), pl.ds(theirs + 1024, 768)], zfb, local_sem.at[0]),
        pltpu.make_async_copy(
            x_ref.at[pl.ds(pl.multiple_of(128 * x, 128), 128), pl.ds(theirs, 1024)], xfb, local_sem.at[1]),
        pltpu.make_async_copy(ct_ref, ct_raw, local_sem.at[2]),
        pltpu.make_async_copy(x_ref.at[:, pl.ds(theirs + 1792, SIDE)], yfb, local_sem.at[3]),
        pltpu.make_async_copy(samples_ref, samples, local_sem.at[4]),
        pltpu.make_async_copy(x_ref.at[:, pl.ds(mine_at, half)], xh, local_sem.at[5]),
        pltpu.make_async_copy(signs_ref, sg, local_sem.at[6]),
    ]
    for load in loads:
        load.start()

    barrier = pltpu.get_barrier_semaphore()
    for d in range(1, 8):
        pl.semaphore_signal(
            barrier, inc=1, device_id=device(wrap(z + d, RING_Z), x, core, tok, probe), device_id_type=MESH)
    for offset in group:
        pl.semaphore_signal(barrier, inc=1, device_id=group_device(offset), device_id_type=MESH)

    numbers = {}
    sent = []

    def number(name):
        return numbers.setdefault(name, len(numbers))

    def send(name, src, dst, target):
        n = number(name)
        copy = pltpu.make_async_remote_copy(
            src_ref=src, dst_ref=dst, send_sem=send_sem.at[n], recv_sem=recv_sem.at[n],
            device_id=target, device_id_type=MESH)
        copy.start()
        sent.append(copy)

    def arrived(name, dst, source):
        n = number(name)
        pltpu.make_async_remote_copy(
            src_ref=dst, dst_ref=dst, send_sem=send_sem.at[n], recv_sem=recv_sem.at[n],
            device_id=source, device_id_type=MESH).wait_recv()

    def xs(k, i):
        return xo.at[core * 8 + k, pl.ds(pl.multiple_of(128 * wrap(i, RING_X), 128), 128)]

    def zs(k, i):
        return xo.at[core * 8 + k, pl.ds(pl.multiple_of(64 * wrap(i, RING_Z), 64), 64)]

    loads[0].wait()
    for j in range(3):
        zf[j] = zfb[:, j * SIDE:(j + 1) * SIDE].astype(F32)
    loads[1].wait()
    for j in range(4):
        xf[j] = xfb[:, j * SIDE:(j + 1) * SIDE].astype(F32)
    loads[2].wait()
    ct_send[...] = ct_raw[...].astype(F32)
    loads[3].wait()
    yf[...] = yfb[...].astype(F32)
    pl.semaphore_wait(barrier, 38)

    route = {}
    for side, k in FEED:
        target = near if side == "n" else far
        if k == "ct":
            send("ct", ct_send, ct_land, target)
        elif k == 7:
            part = pl.ds(0 if side == "n" else 256, 256)
            send(("feed", 7, side), yf.at[part], xo.at[core * 8 + 7, part], target)
        else:
            route[k] = target
            if k < 4:
                send(("feed", k), xf.at[k], xs(k, x), target)
            else:
                send(("feed", k), zf.at[k - 4], zs(k, z), target)

    table[...] = signed_table(SIDE)
    ct_own[...] = jnp.zeros_like(ct_own)
    ct_other[...] = jnp.zeros_like(ct_other)
    ct_own[0:224, :] = ct_raw[...]
    loads[4].wait()
    m = samples[pl.ds(pl.multiple_of(core * 64, 64), 64), :]
    index_v[...] = ((m >> 21 & 1) << 13) | ((m >> 15 & 31) << 8) | (m & 255)
    to_scalar = pltpu.make_async_copy(index_v, index_s, local_sem.at[7])
    to_scalar.start()
    loads[5].wait()
    loads[6].wait()

    def prepare(part):
        def body(i, carry):
            g = 4 * part + i
            even = sg[pl.ds(pl.multiple_of(512 * g, 512), SIDE, stride=2), :]
            odd = sg[pl.ds(pl.multiple_of(512 * g, 512) + 1, SIDE, stride=2), :]
            turned = jnp.concatenate([even.astype(F32).T, odd.astype(F32).T], axis=0)
            product = jnp.dot(
                ct_own[...], xh[:, pl.ds(pl.multiple_of(SIDE * g, SIDE), SIDE)], preferred_element_type=F32)
            sign_t[g] = turned
            base[g] = turned * product
            return carry

        lax.fori_loop(0, 4, body, 0)

    def process(g):
        h = table[...]
        product = jnp.dot(ct_other[...], xo[g].astype(BF16), preferred_element_type=F32)
        high, low = split_two(base[g] + sign_t[g] * product)
        mixed = jnp.dot(h, high, preferred_element_type=F32) + jnp.dot(h, low, preferred_element_type=F32)
        high, low = split_two(mixed)
        mixed = jnp.dot(high, h, preferred_element_type=F32) + jnp.dot(low, h, preferred_element_type=F32)
        f_own[2 * g] = mixed[:, 0:128]
        f_own[2 * g + 1] = mixed[:, 128:256]

    def send_f(name, k, g):
        send((name, k), f_own.at[pl.ds(2 * g, 2)], f_sib.at[pl.ds(2 * g, 2)], sibling)

    def own_chunk(k):
        process(core * 8 + k)
        send_f("f0", k, core * 8 + k)

    def sibling_chunk(k):
        g = (1 - core) * 8 + k
        arrived(("share", k), xo.at[g], sibling)
        process(g)
        send_f("f1", k, g)

    flip = (1 - 2 * core).astype(F32)

    def quad(q):
        for k in (2 * q, 2 * q + 1):
            g = (1 - core) * 8 + k
            arrived(("f0", k), f_sib.at[pl.ds(2 * g, 2)], sibling)
            g = core * 8 + k
            arrived(("f1", k), f_sib.at[pl.ds(2 * g, 2)], sibling)
        blocks = [2 * q, 2 * q + 1, 8 + 2 * q, 9 + 2 * q]

        def body(i, carry):
            part, row = i // 16, pl.multiple_of((i % 16) * 16, 16)
            own = [f_own[2 * g + part, pl.ds(row, 16), :] for g in blocks]
            sib = [f_sib[2 * g + part, pl.ds(row, 16), :] for g in blocks]
            for core_bit in range(2):
                both = [a + b for a, b in zip(own, sib)] if core_bit == 0 else [(a - b) * flip for a, b in zip(own, sib)]
                for g, value in zip(blocks, butterfly(both)):
                    at = (core_bit * 32 + 2 * g + part) * SIDE + row
                    grid[pl.ds(pl.multiple_of(at, 16), 16), :] = value
            return carry

        lax.fori_loop(0, 32, body, 0, unroll=2)

    def take_ct():
        arrived("ct", ct_land, near)
        ct_other[0:224, :] = ct_land[...].astype(BF16)

    def complete(k):
        g = core * 8 + k
        send(("share", k), xo.at[g], xo.at[g], sibling)

    def hop_x(k, d):
        if d == 0:
            arrived(("feed", k), xs(k, x), route[k])
            send(("xr", k), xs(k, x), xs(k, x), right_x)
            send(("xl", k), xs(k, x), xs(k, x), left_x)
        elif d == 1:
            arrived(("xr", k), xs(k, x - 1), left_x)
            if k % 2 == 0:
                send(("xe", k), xs(k, x - 1), xs(k, x - 1), right_x)
            arrived(("xl", k), xs(k, x + 1), right_x)
            if k % 2 == 1:
                send(("xe", k), xs(k, x + 1), xs(k, x + 1), left_x)
        else:
            arrived(("xe", k), xs(k, x + 2), left_x if k % 2 == 0 else right_x)
            complete(k)

    def hop_z(k, d):
        if d == 0:
            arrived(("feed", k), zs(k, z), route[k])
            send(("zr", k, 1), zs(k, z), zs(k, z), right_z)
            send(("zl", k, 1), zs(k, z), zs(k, z), left_z)
        elif d < 4:
            arrived(("zr", k, d), zs(k, z - d), left_z)
            if d < 3 or k % 2 == 0:
                send(("zr", k, d + 1), zs(k, z - d), zs(k, z - d), right_z)
            arrived(("zl", k, d), zs(k, z + d), right_z)
            if d < 3 or k % 2 == 1:
                send(("zl", k, d + 1), zs(k, z + d), zs(k, z + d), left_z)
        else:
            if k % 2 == 0:
                arrived(("zr", k, 4), zs(k, z - 4), left_z)
            else:
                arrived(("zl", k, 4), zs(k, z + 4), right_z)
            complete(k)

    def hop_y(k):
        arrived(("feed", k, "n"), xo.at[core * 8 + k, pl.ds(0, 256)], near)
        arrived(("feed", k, "f"), xo.at[core * 8 + k, pl.ds(256, 256)], far)
        complete(k)

    for step in " ".join(ORDER).split():
        kind, k, d = step[0], int(step[1]), int(step[2])
        if kind == "x":
            hop_x(k, d)
        elif kind == "z":
            hop_z(k, d)
        elif kind == "y":
            hop_y(k)
        elif kind == "c":
            take_ct()
        elif kind == "p":
            prepare(k)
        elif kind == "m":
            own_chunk(k)
        elif kind == "t":
            sibling_chunk(k)
        else:
            quad(k)

    def last(i, carry):
        at = (i // 16) * 16 * SIDE + ((i // 4) % 4) * SIDE + (i % 4) * 64
        for r in range(0, 64, 16):
            places = [pl.ds(pl.multiple_of(at + q * 4 * SIDE + r, 16), 16) for q in range(4)]
            for place, value in zip(places, butterfly([grid[place, :] for place in places])):
                grid[place, :] = value
        return carry

    lax.fori_loop(0, 64, last, 0)
    to_scalar.wait()
    me = x * 2 + tok

    def xt_device(member):
        return device(z, member // 2, core, member % 2, probe)

    def group_source(offset):
        dx, dt, dp, dc = offset
        return wrap(x - dx, RING_X), core ^ dc, tok ^ dt, probe ^ dp

    code = tok | (x << 2) | (z << 4)
    lanes = lax.broadcasted_iota(jnp.int32, (128, 128), 0)

    def gather_piece(piece):
        row0 = core * 64 + piece * 8

        def body(b, carry):
            for k in range(128):
                rows[k:k + 1, :] = grid[pl.ds(index_s[piece * 8 + b, k], 1), :]
            m = samples[pl.ds(row0 + b, 1), :]
            picked = jnp.where(lanes == ((m >> 8) & 127), rows[...].T, 0.0)
            value = jnp.sum(picked, axis=0, keepdims=True)
            odd = (m >> 20) & code
            odd = odd ^ (odd >> 4)
            odd = odd ^ (odd >> 2)
            odd = odd ^ (odd >> 1)
            mine[piece, pl.ds(b, 1), :] = jnp.where((odd & 1) == 1, -value, value)
            return carry

        lax.fori_loop(0, 8, body, 0)

    for d in range(1, 8):
        piece = wrap(me + d, 8)
        gather_piece(piece)
        copy = pltpu.make_async_remote_copy(
            src_ref=mine.at[piece], dst_ref=land_xt.at[d - 1], send_sem=send_small.at[d - 1],
            recv_sem=recv_small.at[d - 1], device_id=xt_device(piece), device_id_type=MESH)
        copy.start()
        sent.append(copy)
    gather_piece(me)
    total = mine[me]
    for d in range(1, 8):
        pltpu.make_async_remote_copy(
            src_ref=land_xt.at[d - 1], dst_ref=land_xt.at[d - 1], send_sem=send_small.at[d - 1],
            recv_sem=recv_small.at[d - 1], device_id=xt_device(wrap(me - d, 8)), device_id_type=MESH).wait_recv()
        total = total + land_xt[d - 1]
    red[...] = total

    def z_copy(source, target):
        return pltpu.make_async_remote_copy(
            src_ref=red, dst_ref=land_z.at[source], send_sem=send_small.at[7 + target],
            recv_sem=recv_small.at[7 + source], device_id=device(target, x, core, tok, probe), device_id_type=MESH)

    for d in range(1, 8):
        copy = z_copy(z, wrap(z + d, RING_Z))
        copy.start()
        sent.append(copy)
    land_z[z] = total
    for d in range(1, 8):
        z_copy(wrap(z - d, RING_Z), z).wait_recv()
    total = land_z[0]
    for i in range(1, 8):
        total = total + land_z[i]
    scale = float(1024 * 134217728) ** (-0.5)

    def place(px, pcore, ptok, pprobe):
        return full.at[pprobe, pl.ds(pl.multiple_of(pcore * 64 + (px * 2 + ptok) * 8, 8), 8)]

    here = place(x, core, tok, probe)
    here[...] = total * scale
    for i, offset in enumerate(group):
        copy = pltpu.make_async_remote_copy(
            src_ref=here, dst_ref=here, send_sem=send_small.at[15 + i], recv_sem=recv_small.at[15 + i],
            device_id=group_device(offset), device_id_type=MESH)
        copy.start()
        sent.append(copy)
    for i, offset in enumerate(group):
        px, pcore, ptok, pprobe = group_source(offset)
        there = place(px, pcore, ptok, pprobe)
        pltpu.make_async_remote_copy(
            src_ref=there, dst_ref=there, send_sem=send_small.at[15 + i], recv_sem=recv_small.at[15 + i],
            device_id=device(z, px, pcore, ptok, pprobe), device_id_type=MESH).wait_recv()

    count = 16384.0

    def mean(value):
        return jnp.sum(jnp.sum(value, axis=0, keepdims=True), axis=1, keepdims=True) / count

    first, second = full[0], full[1]
    unit = first * lax.rsqrt(mean(first * first) + 1e-06)
    rest = second - mean(unit * second) * unit
    last = rest * lax.rsqrt(mean(rest * rest) + 1e-06)
    rows[...] = unit
    start = pl.multiple_of(probe * 64, 64)
    for i in range(64):
        cols = slice(i * 128, (i + 1) * 128)
        sketch_ref[0:1, cols] = full[0, pl.ds(start + i, 1), :]
        sketch_ref[1:2, cols] = full[1, pl.ds(start + i, 1), :]
        basis_ref[0:1, cols] = rows[pl.ds(start + i, 1), :]
    rows[...] = last
    for i in range(64):
        basis_ref[1:2, i * 128:(i + 1) * 128] = rows[pl.ds(start + i, 1), :]
    for copy in sent:
        copy.wait_send()


def whole(tokens_x, cot_t, signs, samples):
    shape = jax.ShapeDtypeStruct((2, 8192), F32)
    return pl.pallas_call(
        whole_kernel,
        out_shape=(shape, shape),
        in_specs=[pl.BlockSpec(memory_space=pl.ANY)] * 4,
        out_specs=(pl.BlockSpec(memory_space=pltpu.VMEM), pl.BlockSpec(memory_space=pltpu.VMEM)),
        scratch_shapes=[
            pltpu.VMEM((512, 4096), BF16),
            pltpu.VMEM((128, 1024), BF16),
            pltpu.VMEM((64, 768), BF16),
            pltpu.VMEM((512, SIDE), BF16),
            pltpu.VMEM((4, 128, SIDE), F32),
            pltpu.VMEM((3, 64, SIDE), F32),
            pltpu.VMEM((512, SIDE), F32),
            pltpu.VMEM((8192, 128), jnp.int32),
            pltpu.VMEM((224, 512), BF16),
            pltpu.VMEM((224, 512), F32),
            pltpu.VMEM((224, 512), F32),
            pltpu.VMEM((SIDE, 512), BF16),
            pltpu.VMEM((SIDE, 512), BF16),
            pltpu.VMEM((SIDE, SIDE), BF16),
            pltpu.VMEM((16, 512, SIDE), F32),
            pltpu.VMEM((16, SIDE, SIDE), F32),
            pltpu.VMEM((16, SIDE, SIDE), F32),
            pltpu.VMEM((32, SIDE, 128), F32),
            pltpu.VMEM((32, SIDE, 128), F32),
            pltpu.VMEM((16384, 128), F32),
            pltpu.VMEM((128, 128), jnp.int32),
            pltpu.VMEM((64, 128), jnp.int32),
            pltpu.SMEM((64, 128), jnp.int32),
            pltpu.VMEM((128, 128), F32),
            pltpu.VMEM((8, 8, 128), F32),
            pltpu.VMEM((7, 8, 128), F32),
            pltpu.VMEM((8, 128), F32),
            pltpu.VMEM((8, 8, 128), F32),
            pltpu.VMEM((2, 128, 128), F32),
            pltpu.SemaphoreType.DMA((8,)),
            pltpu.SemaphoreType.DMA((80,)),
            pltpu.SemaphoreType.DMA((80,)),
            pltpu.SemaphoreType.DMA((46,)),
            pltpu.SemaphoreType.DMA((46,)),
        ],
        compiler_params=pltpu.CompilerParams(
            collective_id=0, has_side_effects=True, vmem_limit_bytes=56 << 20),
        cost_estimate=pl.CostEstimate(flops=8 << 30, bytes_accessed=24 << 20, transcendentals=0),
        name="whole",
    )(tokens_x, cot_t, signs, samples)


def on_device(tokens_x, cotangent, signs, samples):
    return whole(tokens_x, cotangent[0].T, signs.reshape(8192, 128), samples.reshape(128, 128))


def solution(mesh):
    in_specs = (P("tok", None), P("probe", "tok", "param"), P(("param", "tok")), P())
    out_specs = (P(None, "probe"), P(None, "probe"))
    return jax.shard_map(
        on_device, mesh=mesh, in_specs=in_specs, out_specs=out_specs, check_vma=False
    )
```

```python
import functools

import jax
import jax.numpy as jnp
from jax import lax
from jax.experimental import pallas as pl
from jax.experimental.pallas import tpu as pltpu
from jax.sharding import PartitionSpec as P

MESH = pl.DeviceIdType.MESH
RING_X, RING_Z = 4, 8
SIDE = 256
BF16, F32 = jnp.bfloat16, jnp.float32


def position():
    param = lax.axis_index("param")
    z, x, core = param // 8, (param // 2) % 4, param % 2
    return z, x, core, lax.axis_index("tok"), lax.axis_index("probe")


def device(z, x, core, tok, probe):
    return ((z * RING_X + x) * 2 + core, tok, probe)


def wrap(value, size):
    return lax.rem(value + 2 * size, size)


def signed_table(width):
    rows = lax.broadcasted_iota(jnp.int32, (width, width), 0)
    cols = lax.broadcasted_iota(jnp.int32, (width, width), 1)
    bits = rows & cols
    bits = bits ^ (bits >> 4)
    bits = bits ^ (bits >> 2)
    bits = bits ^ (bits >> 1)
    return (1 - 2 * (bits & 1)).astype(F32).astype(BF16)


def split_two(value):
    high = value.astype(BF16)
    return high, (value - high.astype(F32)).astype(BF16)


def butterfly(values):
    values = list(values)
    gap = 1
    while gap < len(values):
        for start in range(0, len(values), 2 * gap):
            for i in range(start, start + gap):
                a, b = values[i], values[i + gap]
                values[i], values[i + gap] = a + b, a - b
        gap *= 2
    return values


FEED = (("n", 1), ("n", 5), ("f", 4), ("f", 2), ("n", "ct"), ("f", 6), ("f", 3), ("n", 7), ("f", 0), ("f", 7))
ORDER = (
    "z40 x10 z50 x20", "z41 z60 p00 z51", "x11 p10 x30 z42", "p20 z61 x21 p30", "x00 z52 z43 x12",
    "c00 z62 z53 x31", "x22 c10 m10 m20", "z44 m40 z63 x01", "z54 m50 y70 m70", "x32 m30 z64 m60",
    "q20 x02 m00 q10", "q30 q00",
)


def whole_kernel(
    x_ref, ct_ref, signs_ref, samples_ref, sketch_ref, basis_ref,
    xh, xfb, zfb, yfb, xf, zf, yf, sg, ct_raw, ct_send, ct_mate, ct_land, ct_own, ct_other, table,
    xo, base, sign_t, grid, samples, index_v, index_s,
    rows, rows_b, mine, land_xt, red, land_z, full,
    local_sem, send_sem, recv_sem, send_small, recv_small,
):
    z, x, core, tok, probe = position()
    half = 4096
    near = device(z, x, core, 1 - tok, probe)
    far = device(z, x, core, 1 - tok, 1 - probe)
    right_x = device(z, wrap(x + 1, RING_X), core, tok, probe)
    left_x = device(z, wrap(x - 1, RING_X), core, tok, probe)
    right_z = device(wrap(z + 1, RING_Z), x, core, tok, probe)
    left_z = device(wrap(z - 1, RING_Z), x, core, tok, probe)
    sibling = device(z, x, 1 - core, tok, probe)
    me = x * 2 + tok

    def xt_device(member):
        return device(z, member // 2, core, member % 2, probe)

    def column_device(other_z, other_core):
        return device(other_z, x, other_core, tok, probe)

    def plane_device(member, other_probe):
        return device(z, member // 2, core, member % 2, other_probe)

    column = [(dz, dc) for dz in range(8) for dc in range(2)][1:]
    plane = [(d, dp) for d in range(8) for dp in range(2)][1:]

    mine_at = pl.multiple_of(tok * half + core * 2048, 128)
    theirs = pl.multiple_of((1 - tok) * half + core * 2048, 128)
    loads = [
        pltpu.make_async_copy(
            x_ref.at[pl.ds(pl.multiple_of(64 * z, 64), 64), pl.ds(theirs + 1024, 768)], zfb, local_sem.at[0]),
        pltpu.make_async_copy(
            x_ref.at[pl.ds(pl.multiple_of(128 * x, 128), 128), pl.ds(theirs, 1024)], xfb, local_sem.at[1]),
        pltpu.make_async_copy(ct_ref, ct_raw, local_sem.at[2]),
        pltpu.make_async_copy(x_ref.at[:, pl.ds(theirs + 1792, SIDE)], yfb, local_sem.at[3]),
        pltpu.make_async_copy(samples_ref, samples, local_sem.at[4]),
        pltpu.make_async_copy(x_ref.at[:, pl.ds(mine_at, 2048)], xh, local_sem.at[5]),
        pltpu.make_async_copy(
            signs_ref.at[pl.ds(pl.multiple_of(core * half, half), half)], sg.at[core], local_sem.at[6]),
    ]
    for load in loads:
        load.start()

    barrier = pltpu.get_barrier_semaphore()
    partners = [plane_device(wrap(me + d, 8), probe ^ dp) for d, dp in plane]
    partners += [column_device(wrap(z + dz, 8), core ^ dc) for dz, dc in column]
    for partner in partners:
        pl.semaphore_signal(barrier, inc=1, device_id=partner, device_id_type=MESH)

    numbers = {}
    sent = []

    def number(name):
        return numbers.setdefault(name, len(numbers))

    def send(name, src, dst, target):
        n = number(name)
        copy = pltpu.make_async_remote_copy(
            src_ref=src, dst_ref=dst, send_sem=send_sem.at[n], recv_sem=recv_sem.at[n],
            device_id=target, device_id_type=MESH)
        copy.start()
        sent.append(copy)
        return copy

    def arrived(name, dst, source):
        n = number(name)
        pltpu.make_async_remote_copy(
            src_ref=dst, dst_ref=dst, send_sem=send_sem.at[n], recv_sem=recv_sem.at[n],
            device_id=source, device_id_type=MESH).wait_recv()

    def xs(k, i):
        return xo.at[k, pl.ds(pl.multiple_of(128 * wrap(i, RING_X), 128), 128)]

    def zs(k, i):
        return xo.at[k, pl.ds(pl.multiple_of(64 * wrap(i, RING_Z), 64), 64)]

    loads[0].wait()
    for j in range(3):
        zf[j] = zfb[:, j * SIDE:(j + 1) * SIDE].astype(F32)
    loads[1].wait()
    for j in range(4):
        xf[j] = xfb[:, j * SIDE:(j + 1) * SIDE].astype(F32)
    pl.semaphore_wait(barrier, len(partners))

    route = {}
    for side, k in FEED:
        target = near if side == "n" else far
        if k == "ct":
            loads[2].wait()
            ct_send[...] = ct_raw[...].astype(F32)
            send("ct", ct_send, ct_land.at[core], target)
        elif k == 7:
            if side == "n":
                loads[3].wait()
                yf[...] = yfb[...].astype(F32)
            part = pl.ds(0 if side == "n" else 256, 256)
            send(("feed", 7, side), yf.at[part], xo.at[7, part], target)
        else:
            route[k] = target
            if k < 4:
                send(("feed", k), xf.at[k], xs(k, x), target)
            else:
                send(("feed", k), zf.at[k - 4], zs(k, z), target)

    send("mate", ct_send, ct_mate, sibling)
    send("signs", signs_ref.at[pl.ds(pl.multiple_of((1 - core) * half, half), half)], sg.at[core], sibling)
    table[...] = signed_table(SIDE)
    ct_own[...] = jnp.zeros_like(ct_own)
    ct_other[...] = jnp.zeros_like(ct_other)
    own_rows = pl.ds(pl.multiple_of(core * SIDE, SIDE), 224)
    mate_rows = pl.ds(pl.multiple_of((1 - core) * SIDE, SIDE), 224)
    ct_own[own_rows, :] = ct_raw[...]
    loads[4].wait()
    m = samples[pl.ds(pl.multiple_of(core * 64, 64), 64), :]
    index_v[...] = ((m >> 16 & 15) << 10) | ((m >> 21 & 1) << 9) | ((m >> 15 & 1) << 8) | (m & 255)
    to_scalar = pltpu.make_async_copy(index_v, index_s, local_sem.at[7])
    to_scalar.start()
    loads[5].wait()
    loads[6].wait()
    arrived("mate", ct_mate, sibling)
    ct_own[mate_rows, :] = ct_mate[...].astype(BF16)
    arrived("signs", sg.at[1 - core], sibling)

    def prepare(part):
        def body(i, carry):
            k = 2 * part + i
            product = jnp.dot(
                ct_own[...], xh[:, pl.ds(pl.multiple_of(SIDE * k, SIDE), SIDE)], preferred_element_type=F32)
            for b in range(2):
                even = sg[b, pl.ds(pl.multiple_of(512 * k, 512), SIDE, stride=2), :]
                odd = sg[b, pl.ds(pl.multiple_of(512 * k, 512) + 1, SIDE, stride=2), :]
                turned = jnp.concatenate([even.astype(F32).T, odd.astype(F32).T], axis=0)
                rows_b = slice(b * SIDE, (b + 1) * SIDE)
                sign_t[k, rows_b, :] = turned
                base[k, rows_b, :] = turned * product[rows_b]
            return carry

        lax.fori_loop(0, 2, body, 0)

    def place_of(g, sel):
        return grid.at[pl.ds(pl.multiple_of(g * 1024 + sel * 512, 512), 512)]

    sent_grid = {}

    def process(k):
        h = table[...]
        product = jnp.dot(ct_other[...], xo[k].astype(BF16), preferred_element_type=F32)
        value = base[k] + sign_t[k] * product
        at = (core * 8 + k) * 1024
        for sel in range(2):
            both = value[:SIDE] + value[SIDE:] if sel == 0 else value[:SIDE] - value[SIDE:]
            high, low = split_two(both)
            mixed = jnp.dot(h, high, preferred_element_type=F32) + jnp.dot(h, low, preferred_element_type=F32)
            high, low = split_two(mixed)
            mixed = jnp.dot(high, h, preferred_element_type=F32) + jnp.dot(low, h, preferred_element_type=F32)
            for part in range(2):
                first_row = pl.multiple_of(at + (sel * 2 + part) * SIDE, SIDE)
                grid[pl.ds(first_row, SIDE), :] = mixed[:, part * 128:(part + 1) * 128]
            place = place_of(core * 8 + k, sel)
            sent_grid[k, sel] = send(("grid", k, sel), place, place, sibling)

    def quad(q):
        for k in (2 * q, 2 * q + 1):
            for sel in range(2):
                arrived(("grid", k, sel), place_of((1 - core) * 8 + k, sel), sibling)
                sent_grid[k, sel].wait_send()
                sent[:] = [copy for copy in sent if copy is not sent_grid[k, sel]]

        def body(i, carry):
            rows_of = [
                [pl.ds(pl.multiple_of(g * 1024 + i * 64 + r, 16), 16) for g in (2 * q, 2 * q + 1, 8 + 2 * q, 9 + 2 * q)]
                for r in range(0, 64, 16)]
            values = [butterfly([grid[place, :] for place in places]) for places in rows_of]
            for places, results in zip(rows_of, values):
                for place, result in zip(places, results):
                    grid[place, :] = result
            return carry

        lax.fori_loop(0, 16, body, 0)

    def take_ct(step):
        if step == 0:
            arrived("ct", ct_land.at[core], near)
            send("ct2", ct_land.at[core], ct_land.at[core], sibling)
            ct_other[own_rows, :] = ct_land[core].astype(BF16)
        else:
            arrived("ct2", ct_land.at[1 - core], sibling)
            ct_other[mate_rows, :] = ct_land[1 - core].astype(BF16)

    def hop_x(k, d):
        if d == 0:
            arrived(("feed", k), xs(k, x), route[k])
            send(("xr", k), xs(k, x), xs(k, x), right_x)
            send(("xl", k), xs(k, x), xs(k, x), left_x)
        elif d == 1:
            arrived(("xr", k), xs(k, x - 1), left_x)
            if k % 2 == 0:
                send(("xe", k), xs(k, x - 1), xs(k, x - 1), right_x)
            arrived(("xl", k), xs(k, x + 1), right_x)
            if k % 2 == 1:
                send(("xe", k), xs(k, x + 1), xs(k, x + 1), left_x)
        else:
            arrived(("xe", k), xs(k, x + 2), left_x if k % 2 == 0 else right_x)

    def hop_z(k, d):
        if d == 0:
            arrived(("feed", k), zs(k, z), route[k])
            send(("zr", k, 1), zs(k, z), zs(k, z), right_z)
            send(("zl", k, 1), zs(k, z), zs(k, z), left_z)
        elif d < 4:
            arrived(("zr", k, d), zs(k, z - d), left_z)
            if d < 3 or k % 2 == 0:
                send(("zr", k, d + 1), zs(k, z - d), zs(k, z - d), right_z)
            arrived(("zl", k, d), zs(k, z + d), right_z)
            if d < 3 or k % 2 == 1:
                send(("zl", k, d + 1), zs(k, z + d), zs(k, z + d), left_z)
        else:
            if k % 2 == 0:
                arrived(("zr", k, 4), zs(k, z - 4), left_z)
            else:
                arrived(("zl", k, 4), zs(k, z + 4), right_z)

    def hop_y(k):
        arrived(("feed", k, "n"), xo.at[k, pl.ds(0, 256)], near)
        arrived(("feed", k, "f"), xo.at[k, pl.ds(256, 256)], far)

    for step in " ".join(ORDER).split():
        kind, k, d = step[0], int(step[1]), int(step[2])
        if kind == "x":
            hop_x(k, d)
        elif kind == "z":
            hop_z(k, d)
        elif kind == "y":
            hop_y(k)
        elif kind == "c":
            take_ct(k)
        elif kind == "p":
            prepare(k)
        elif kind == "m":
            process(k)
        else:
            quad(k)

    def last(i, carry):
        at = (i // 32) * 8192 + (i // 16 % 2) * 1024 + (i % 16) * 64
        rows_of = [
            [pl.ds(pl.multiple_of(at + q * 2048 + r, 16), 16) for q in range(4)] for r in range(0, 64, 16)]
        values = [butterfly([grid[place, :] for place in places]) for places in rows_of]
        for places, results in zip(rows_of, values):
            for place, result in zip(places, results):
                grid[place, :] = result
        return carry

    lax.fori_loop(0, 64, last, 0)
    to_scalar.wait()
    code = tok | (x << 2) | (z << 4)
    lanes = lax.broadcasted_iota(jnp.int32, (128, 128), 0)

    def place_in(n):
        return wrap(me + 1 + n // 8, 8), n % 8

    def gather(n, to):
        piece, b = place_in(n)
        for r in range(0, 128, 8):
            to[r:r + 8, :] = jnp.concatenate(
                [grid[pl.ds(index_s[piece * 8 + b, r + k], 1), :] for k in range(8)], axis=0)

    def pick(n, got):
        piece, b = place_in(n)
        m = samples[pl.ds(core * 64 + piece * 8 + b, 1), :]
        picked = jnp.where(lanes == ((m >> 8) & 127), got[...].T, 0.0)
        value = jnp.sum(picked, axis=0, keepdims=True)
        odd = (m >> 20) & code
        odd = odd ^ (odd >> 4)
        odd = odd ^ (odd >> 2)
        odd = odd ^ (odd >> 1)
        mine[piece, pl.ds(b, 1), :] = jnp.where((odd & 1) == 1, -value, value)

    def xt_copy(d, piece, member):
        return pltpu.make_async_remote_copy(
            src_ref=mine.at[piece], dst_ref=land_xt.at[d - 1], send_sem=send_small.at[d - 1],
            recv_sem=recv_small.at[d - 1], device_id=xt_device(member), device_id_type=MESH)

    def gather_step(i, carry):
        gather(2 * i + 1, rows_b)
        pick(2 * i, rows)
        gather(jnp.minimum(2 * i + 2, 63), rows)
        pick(2 * i + 1, rows_b)

        @pl.when(jnp.logical_and(i % 4 == 3, i < 28))
        def _():
            d = i // 4 + 1
            piece = wrap(me + d, 8)
            xt_copy(d, piece, piece).start()

        return carry

    gather(0, rows)
    lax.fori_loop(0, 32, gather_step, 0)
    total = mine[me]
    for d in range(1, 8):
        xt_copy(d, wrap(me + d, 8), wrap(me - d, 8)).wait_recv()
        total = total + land_xt[d - 1]
    red[...] = total

    def column_copy(source, target):
        return pltpu.make_async_remote_copy(
            src_ref=red, dst_ref=land_z.at[source], send_sem=send_small.at[7 + target],
            recv_sem=recv_small.at[7 + source], device_id=column_device(target // 2, target % 2), device_id_type=MESH)

    here = z * 2 + core
    for dz, dc in column:
        copy = column_copy(here, wrap(z + dz, 8) * 2 + (core ^ dc))
        copy.start()
        sent.append(copy)
    land_z[here] = total
    for dz, dc in column:
        column_copy(wrap(z - dz, 8) * 2 + (core ^ dc), here).wait_recv()
    scale = float(1024 * 134217728) ** (-0.5)

    for c in range(2):
        total = land_z[c]
        for i in range(1, 8):
            total = total + land_z[2 * i + c]
        full[me, probe, c] = total * scale

    def plane_copy(n, row, row_probe, member, other_probe):
        place = full.at[row, row_probe]
        return pltpu.make_async_remote_copy(
            src_ref=place, dst_ref=place, send_sem=send_small.at[23 + n], recv_sem=recv_small.at[23 + n],
            device_id=plane_device(member, other_probe), device_id_type=MESH)

    for n, (d, dp) in enumerate(plane):
        copy = plane_copy(n, me, probe, wrap(me + d, 8), probe ^ dp)
        copy.start()
        sent.append(copy)
    for n, (d, dp) in enumerate(plane):
        source = wrap(me - d, 8)
        plane_copy(n, source, probe ^ dp, source, probe ^ dp).wait_recv()

    count = 16384.0

    def mean(value):
        value = jnp.sum(value, axis=(0, 1))
        return jnp.sum(jnp.sum(value, axis=0, keepdims=True), axis=1, keepdims=True) / count

    first, second = full[:, 0], full[:, 1]
    unit = first * lax.rsqrt(mean(first * first) + 1e-06)
    rest = second - mean(unit * second) * unit
    last = rest * lax.rsqrt(mean(rest * rest) + 1e-06)
    by_probe = probe == 0
    for i in range(8):
        at = slice(i * 8, (i + 1) * 8)
        sketch_ref[0, at, :] = jnp.where(by_probe, first[i, 0], first[i, 1])
        sketch_ref[1, at, :] = jnp.where(by_probe, second[i, 0], second[i, 1])
        basis_ref[0, at, :] = jnp.where(by_probe, unit[i, 0], unit[i, 1])
        basis_ref[1, at, :] = jnp.where(by_probe, last[i, 0], last[i, 1])
    for d in range(1, 8):
        xt_copy(d, wrap(me + d, 8), wrap(me + d, 8)).wait_send()
    for copy in sent:
        copy.wait_send()


def whole(tokens_x, cot_t, signs, samples):
    shape = jax.ShapeDtypeStruct((2, 64, 128), F32)
    return pl.pallas_call(
        whole_kernel,
        out_shape=(shape, shape),
        in_specs=[pl.BlockSpec(memory_space=pltpu.HBM)] * 4,
        out_specs=(pl.BlockSpec(memory_space=pltpu.VMEM), pl.BlockSpec(memory_space=pltpu.VMEM)),
        scratch_shapes=[
            pltpu.VMEM((512, 2048), BF16),
            pltpu.VMEM((128, 1024), BF16),
            pltpu.VMEM((64, 768), BF16),
            pltpu.VMEM((512, SIDE), BF16),
            pltpu.VMEM((4, 128, SIDE), F32),
            pltpu.VMEM((3, 64, SIDE), F32),
            pltpu.VMEM((512, SIDE), F32),
            pltpu.VMEM((2, 4096, 128), jnp.int32),
            pltpu.VMEM((224, 512), BF16),
            pltpu.VMEM((224, 512), F32),
            pltpu.VMEM((224, 512), F32),
            pltpu.VMEM((2, 224, 512), F32),
            pltpu.VMEM((512, 512), BF16),
            pltpu.VMEM((512, 512), BF16),
            pltpu.VMEM((SIDE, SIDE), BF16),
            pltpu.VMEM((8, 512, SIDE), F32),
            pltpu.VMEM((8, 512, SIDE), F32),
            pltpu.VMEM((8, 512, SIDE), F32),
            pltpu.VMEM((16384, 128), F32),
            pltpu.VMEM((128, 128), jnp.int32),
            pltpu.VMEM((64, 128), jnp.int32),
            pltpu.SMEM((64, 128), jnp.int32),
            pltpu.VMEM((128, 128), F32),
            pltpu.VMEM((128, 128), F32),
            pltpu.VMEM((8, 8, 128), F32),
            pltpu.VMEM((7, 8, 128), F32),
            pltpu.VMEM((8, 128), F32),
            pltpu.VMEM((16, 8, 128), F32),
            pltpu.VMEM((8, 2, 2, 8, 128), F32),
            pltpu.SemaphoreType.DMA((8,)),
            pltpu.SemaphoreType.DMA((88,)),
            pltpu.SemaphoreType.DMA((88,)),
            pltpu.SemaphoreType.DMA((38,)),
            pltpu.SemaphoreType.DMA((38,)),
        ],
        compiler_params=pltpu.CompilerParams(
            collective_id=0, has_side_effects=True, vmem_limit_bytes=56 << 20),
        cost_estimate=pl.CostEstimate(flops=8 << 30, bytes_accessed=24 << 20, transcendentals=0),
        name="whole",
    )(tokens_x, cot_t, signs, samples)


def on_device(tokens_x, cotangent, signs, samples):
    sketch, basis = whole(tokens_x, cotangent[0].T, signs.reshape(8192, 128), samples.reshape(128, 128))
    return sketch.reshape(2, 8192), basis.reshape(2, 8192)


def solution(mesh):
    in_specs = (P("tok", None), P("probe", "tok", "param"), P(("param", "tok")), P())
    out_specs = (P(None, "probe"), P(None, "probe"))
    return jax.shard_map(
        on_device, mesh=mesh, in_specs=in_specs, out_specs=out_specs, check_vma=False
    )
```

```python
import functools

import jax
import jax.numpy as jnp
from jax import lax
from jax.experimental import pallas as pl
from jax.experimental.pallas import tpu as pltpu
from jax.sharding import PartitionSpec as P

MESH = pl.DeviceIdType.MESH
RING_X, RING_Z = 4, 8
SIDE = 256
BF16, F32 = jnp.bfloat16, jnp.float32


def position():
    param = lax.axis_index("param")
    z, x, core = param // 8, (param // 2) % 4, param % 2
    return z, x, core, lax.axis_index("tok"), lax.axis_index("probe")


def device(z, x, core, tok, probe):
    return ((z * RING_X + x) * 2 + core, tok, probe)


def wrap(value, size):
    return lax.rem(value + 2 * size, size)


def signed_table(width):
    rows = lax.broadcasted_iota(jnp.int32, (width, width), 0)
    cols = lax.broadcasted_iota(jnp.int32, (width, width), 1)
    bits = rows & cols
    bits = bits ^ (bits >> 4)
    bits = bits ^ (bits >> 2)
    bits = bits ^ (bits >> 1)
    return (1 - 2 * (bits & 1)).astype(F32).astype(BF16)


def split_two(value):
    high = value.astype(BF16)
    return high, (value - high.astype(F32)).astype(BF16)


def butterfly(values):
    values = list(values)
    gap = 1
    while gap < len(values):
        for start in range(0, len(values), 2 * gap):
            for i in range(start, start + gap):
                a, b = values[i], values[i + gap]
                values[i], values[i + gap] = a + b, a - b
        gap *= 2
    return values


FEED = (("n", 1), ("n", 5), ("f", 4), ("f", 2), ("n", "ct"), ("f", 6), ("f", 3), ("n", 7), ("f", 0), ("f", 7))
ORDER = (
    "z40 x10 z50 x20", "z41 z60 p00 z51", "x11 p10 x30 z42", "p20 z61 x21 p30", "x00 z52 z43 x12",
    "c00 z62 z53 x31", "x22 c10 m10 m20", "z44 m40 z63 x01", "z54 m50 y70 m70", "x32 m30 z64 m60",
    "q20 x02 m00 q10", "q30 q00",
)


def whole_kernel(
    x_ref, ct_ref, signs_ref, samples_ref, sketch_ref, basis_ref,
    xh, xfb, zfb, yfb, xf, zf, yf, sg, ct_raw, ct_send, ct_mate, ct_land, ct_own, ct_other, table,
    xo, base, sign_t, grid, samples, index_v, index_s,
    rows, rows_b, mine, land_xt, red, land_z, full,
    local_sem, send_sem, recv_sem, send_small, recv_small,
):
    z, x, core, tok, probe = position()
    half = 4096
    near = device(z, x, core, 1 - tok, probe)
    far = device(z, x, core, 1 - tok, 1 - probe)
    right_x = device(z, wrap(x + 1, RING_X), core, tok, probe)
    left_x = device(z, wrap(x - 1, RING_X), core, tok, probe)
    right_z = device(wrap(z + 1, RING_Z), x, core, tok, probe)
    left_z = device(wrap(z - 1, RING_Z), x, core, tok, probe)
    sibling = device(z, x, 1 - core, tok, probe)
    me = x * 2 + tok

    def xt_device(member):
        return device(z, member // 2, core, member % 2, probe)

    def column_device(other_z, other_core):
        return device(other_z, x, other_core, tok, probe)

    def plane_device(member, other_probe):
        return device(z, member // 2, core, member % 2, other_probe)

    column = [(dz, dc) for dz in (4, 3, 5, 2, 6, 1, 7, 0) for dc in (1, 0)][:-1]
    plane = [(d, dp) for d in (4, 5, 3, 2, 6, 7, 1, 0) for dp in (1, 0)][:-1]

    mine_at = pl.multiple_of(tok * half + core * 2048, 128)
    theirs = pl.multiple_of((1 - tok) * half + core * 2048, 128)
    loads = [
        pltpu.make_async_copy(
            x_ref.at[pl.ds(pl.multiple_of(64 * z, 64), 64), pl.ds(theirs + 1024, 768)], zfb, local_sem.at[0]),
        pltpu.make_async_copy(
            x_ref.at[pl.ds(pl.multiple_of(128 * x, 128), 128), pl.ds(theirs, 1024)], xfb, local_sem.at[1]),
        pltpu.make_async_copy(ct_ref, ct_raw, local_sem.at[2]),
        pltpu.make_async_copy(x_ref.at[:, pl.ds(theirs + 1792, SIDE)], yfb, local_sem.at[3]),
        pltpu.make_async_copy(samples_ref, samples, local_sem.at[4]),
        pltpu.make_async_copy(x_ref.at[:, pl.ds(mine_at, 2048)], xh, local_sem.at[5]),
        pltpu.make_async_copy(
            signs_ref.at[pl.ds(pl.multiple_of(core * half, half), half)], sg.at[core], local_sem.at[6]),
    ]
    for load in loads:
        load.start()

    barrier = pltpu.get_barrier_semaphore()
    partners = [plane_device(wrap(me + d, 8), probe ^ dp) for d, dp in plane]
    partners += [column_device(wrap(z + dz, 8), core ^ dc) for dz, dc in column]
    for partner in partners:
        pl.semaphore_signal(barrier, inc=1, device_id=partner, device_id_type=MESH)

    numbers = {}
    sent = []

    def number(name):
        return numbers.setdefault(name, len(numbers))

    def send(name, src, dst, target):
        n = number(name)
        copy = pltpu.make_async_remote_copy(
            src_ref=src, dst_ref=dst, send_sem=send_sem.at[n], recv_sem=recv_sem.at[n],
            device_id=target, device_id_type=MESH)
        copy.start()
        sent.append(copy)
        return copy

    def arrived(name, dst, source):
        n = number(name)
        pltpu.make_async_remote_copy(
            src_ref=dst, dst_ref=dst, send_sem=send_sem.at[n], recv_sem=recv_sem.at[n],
            device_id=source, device_id_type=MESH).wait_recv()

    def xs(k, i):
        return xo.at[k, pl.ds(pl.multiple_of(128 * wrap(i, RING_X), 128), 128)]

    def xs_part(k, i, part):
        return xo.at[k, pl.ds(pl.multiple_of(128 * wrap(i, RING_X) + part, 64), 64)]

    def zs(k, i):
        return xo.at[k, pl.ds(pl.multiple_of(64 * wrap(i, RING_Z), 64), 64)]

    loads[0].wait()
    for j in range(3):
        zf[j] = zfb[:, j * SIDE:(j + 1) * SIDE].astype(F32)
    loads[1].wait()
    for j in range(4):
        xf[j] = xfb[:, j * SIDE:(j + 1) * SIDE].astype(F32)
    pl.semaphore_wait(barrier, len(partners))

    route = {}
    split = {k for _, k in FEED if k != 7 and sum(entry[1] == k for entry in FEED) == 2}
    for side, k in FEED:
        target = near if side == "n" else far
        if k == "ct":
            loads[2].wait()
            ct_send[...] = ct_raw[...].astype(F32)
            send("ct", ct_send, ct_land.at[core], target)
        elif k == 7:
            if side == "n":
                loads[3].wait()
                yf[...] = yfb[...].astype(F32)
            part = pl.ds(0 if side == "n" else 256, 256)
            send(("feed", 7, side), yf.at[part], xo.at[7, part], target)
        else:
            route[k] = target
            if k in split:
                part = 0 if side == "n" else 64
                send(("feed", k, side), xf.at[k, pl.ds(part, 64)], xs_part(k, x, part), target)
            elif k < 4:
                send(("feed", k), xf.at[k], xs(k, x), target)
            else:
                send(("feed", k), zf.at[k - 4], zs(k, z), target)

    send("mate", ct_send, ct_mate, sibling)
    send("signs", signs_ref.at[pl.ds(pl.multiple_of((1 - core) * half, half), half)], sg.at[core], sibling)
    table[...] = signed_table(SIDE)
    ct_own[...] = jnp.zeros_like(ct_own)
    ct_other[...] = jnp.zeros_like(ct_other)
    own_rows = pl.ds(pl.multiple_of(core * SIDE, SIDE), 224)
    mate_rows = pl.ds(pl.multiple_of((1 - core) * SIDE, SIDE), 224)
    ct_own[own_rows, :] = ct_raw[...]
    loads[4].wait()
    m = samples[pl.ds(pl.multiple_of(core * 64, 64), 64), :]
    index_v[...] = ((m >> 16 & 15) << 10) | ((m >> 21 & 1) << 9) | ((m >> 15 & 1) << 8) | (m & 255)
    to_scalar = pltpu.make_async_copy(index_v, index_s, local_sem.at[7])
    to_scalar.start()
    loads[5].wait()
    loads[6].wait()
    arrived("mate", ct_mate, sibling)
    ct_own[mate_rows, :] = ct_mate[...].astype(BF16)
    arrived("signs", sg.at[1 - core], sibling)

    def prepare(part):
        def body(i, carry):
            k = 2 * part + i
            product = jnp.dot(
                ct_own[...], xh[:, pl.ds(pl.multiple_of(SIDE * k, SIDE), SIDE)], preferred_element_type=F32)
            for b in range(2):
                even = sg[b, pl.ds(pl.multiple_of(512 * k, 512), SIDE, stride=2), :]
                odd = sg[b, pl.ds(pl.multiple_of(512 * k, 512) + 1, SIDE, stride=2), :]
                turned = jnp.concatenate([even.astype(F32).T, odd.astype(F32).T], axis=0)
                rows_b = slice(b * SIDE, (b + 1) * SIDE)
                sign_t[k, rows_b, :] = turned
                base[k, rows_b, :] = turned * product[rows_b]
            return carry

        lax.fori_loop(0, 2, body, 0)

    def place_of(g, sel):
        return grid.at[pl.ds(pl.multiple_of(g * 1024 + sel * 512, 512), 512)]

    sent_grid = {}

    def process(k):
        h = table[...]
        product = jnp.dot(ct_other[...], xo[k].astype(BF16), preferred_element_type=F32)
        value = base[k] + sign_t[k] * product
        at = (core * 8 + k) * 1024
        for sel in range(2):
            both = value[:SIDE] + value[SIDE:] if sel == 0 else value[:SIDE] - value[SIDE:]
            high, low = split_two(both)
            mixed = jnp.dot(h, high, preferred_element_type=F32) + jnp.dot(h, low, preferred_element_type=F32)
            high, low = split_two(mixed)
            mixed = jnp.dot(high, h, preferred_element_type=F32) + jnp.dot(low, h, preferred_element_type=F32)
            for part in range(2):
                first_row = pl.multiple_of(at + (sel * 2 + part) * SIDE, SIDE)
                grid[pl.ds(first_row, SIDE), :] = mixed[:, part * 128:(part + 1) * 128]
            place = place_of(core * 8 + k, sel)
            sent_grid[k, sel] = send(("grid", k, sel), place, place, sibling)

    def quad(q):
        for k in (2 * q, 2 * q + 1):
            for sel in range(2):
                arrived(("grid", k, sel), place_of((1 - core) * 8 + k, sel), sibling)
                sent_grid[k, sel].wait_send()
                sent[:] = [copy for copy in sent if copy is not sent_grid[k, sel]]

        def body(i, carry):
            rows_of = [
                [pl.ds(pl.multiple_of(g * 1024 + i * 64 + r, 16), 16) for g in (2 * q, 2 * q + 1, 8 + 2 * q, 9 + 2 * q)]
                for r in range(0, 64, 16)]
            values = [butterfly([grid[place, :] for place in places]) for places in rows_of]
            for places, results in zip(rows_of, values):
                for place, result in zip(places, results):
                    grid[place, :] = result
            return carry

        lax.fori_loop(0, 16, body, 0, unroll=4)

    def take_ct(step):
        if step == 0:
            arrived("ct", ct_land.at[core], near)
            send("ct2", ct_land.at[core], ct_land.at[core], sibling)
            ct_other[own_rows, :] = ct_land[core].astype(BF16)
        else:
            arrived("ct2", ct_land.at[1 - core], sibling)
            ct_other[mate_rows, :] = ct_land[1 - core].astype(BF16)

    def hop_x(k, d):
        if d == 0:
            if k in split:
                arrived(("feed", k, "n"), xs_part(k, x, 0), near)
                arrived(("feed", k, "f"), xs_part(k, x, 64), far)
            else:
                arrived(("feed", k), xs(k, x), route[k])
            send(("xr", k), xs(k, x), xs(k, x), right_x)
            send(("xl", k), xs(k, x), xs(k, x), left_x)
        elif d == 1:
            arrived(("xr", k), xs(k, x - 1), left_x)
            if k % 2 == 0:
                send(("xe", k), xs(k, x - 1), xs(k, x - 1), right_x)
            arrived(("xl", k), xs(k, x + 1), right_x)
            if k % 2 == 1:
                send(("xe", k), xs(k, x + 1), xs(k, x + 1), left_x)
        else:
            arrived(("xe", k), xs(k, x + 2), left_x if k % 2 == 0 else right_x)

    def hop_z(k, d):
        if d == 0:
            arrived(("feed", k), zs(k, z), route[k])
            send(("zr", k, 1), zs(k, z), zs(k, z), right_z)
            send(("zl", k, 1), zs(k, z), zs(k, z), left_z)
        elif d < 4:
            arrived(("zr", k, d), zs(k, z - d), left_z)
            if d < 3 or k % 2 == 0:
                send(("zr", k, d + 1), zs(k, z - d), zs(k, z - d), right_z)
            arrived(("zl", k, d), zs(k, z + d), right_z)
            if d < 3 or k % 2 == 1:
                send(("zl", k, d + 1), zs(k, z + d), zs(k, z + d), left_z)
        else:
            if k % 2 == 0:
                arrived(("zr", k, 4), zs(k, z - 4), left_z)
            else:
                arrived(("zl", k, 4), zs(k, z + 4), right_z)

    def hop_y(k):
        arrived(("feed", k, "n"), xo.at[k, pl.ds(0, 256)], near)
        arrived(("feed", k, "f"), xo.at[k, pl.ds(256, 256)], far)

    for step in " ".join(ORDER).split():
        kind, k, d = step[0], int(step[1]), int(step[2])
        if kind == "x":
            hop_x(k, d)
        elif kind == "z":
            hop_z(k, d)
        elif kind == "y":
            hop_y(k)
        elif kind == "c":
            take_ct(k)
        elif kind == "p":
            prepare(k)
        elif kind == "m":
            process(k)
        else:
            quad(k)

    def last(i, carry):
        at = (i // 32) * 8192 + (i // 16 % 2) * 1024 + (i % 16) * 64
        rows_of = [
            [pl.ds(pl.multiple_of(at + q * 2048 + r, 16), 16) for q in range(4)] for r in range(0, 64, 16)]
        values = [butterfly([grid[place, :] for place in places]) for places in rows_of]
        for places, results in zip(rows_of, values):
            for place, result in zip(places, results):
                grid[place, :] = result
        return carry

    lax.fori_loop(0, 64, last, 0, unroll=4)
    to_scalar.wait()
    code = tok | (x << 2) | (z << 4)
    lanes = lax.broadcasted_iota(jnp.int32, (128, 128), 0)

    def place_in(n):
        return wrap(me + 1 + n // 8, 8), n % 8

    def gather(n, to):
        piece, b = place_in(n)
        for r in range(0, 128, 8):
            to[r:r + 8, :] = jnp.concatenate(
                [grid[pl.ds(index_s[piece * 8 + b, r + k], 1), :] for k in range(8)], axis=0)

    def pick(n, got):
        piece, b = place_in(n)
        m = samples[pl.ds(core * 64 + piece * 8 + b, 1), :]
        picked = jnp.where(lanes == ((m >> 8) & 127), got[...].T, 0.0)
        value = jnp.sum(picked, axis=0, keepdims=True)
        odd = (m >> 20) & code
        odd = odd ^ (odd >> 4)
        odd = odd ^ (odd >> 2)
        odd = odd ^ (odd >> 1)
        mine[piece, pl.ds(b, 1), :] = jnp.where((odd & 1) == 1, -value, value)

    def xt_copy(d, piece, member):
        return pltpu.make_async_remote_copy(
            src_ref=mine.at[piece], dst_ref=land_xt.at[d - 1], send_sem=send_small.at[d - 1],
            recv_sem=recv_small.at[d - 1], device_id=xt_device(member), device_id_type=MESH)

    def gather_step(i, carry):
        gather(2 * i + 1, rows_b)
        pick(2 * i, rows)
        gather(jnp.minimum(2 * i + 2, 63), rows)
        pick(2 * i + 1, rows_b)

        @pl.when(jnp.logical_and(i % 4 == 3, i < 28))
        def _():
            d = i // 4 + 1
            piece = wrap(me + d, 8)
            xt_copy(d, piece, piece).start()

        return carry

    gather(0, rows)
    lax.fori_loop(0, 32, gather_step, 0)
    total = mine[me]
    for d in range(1, 8):
        xt_copy(d, wrap(me + d, 8), wrap(me - d, 8)).wait_recv()
        total = total + land_xt[d - 1]
    red[...] = total

    def column_copy(source, target):
        return pltpu.make_async_remote_copy(
            src_ref=red, dst_ref=land_z.at[source], send_sem=send_small.at[7 + target],
            recv_sem=recv_small.at[7 + source], device_id=column_device(target // 2, target % 2), device_id_type=MESH)

    here = z * 2 + core
    for dz, dc in column:
        copy = column_copy(here, wrap(z + dz, 8) * 2 + (core ^ dc))
        copy.start()
        sent.append(copy)
    land_z[here] = total
    for dz, dc in column:
        column_copy(wrap(z - dz, 8) * 2 + (core ^ dc), here).wait_recv()
    scale = float(1024 * 134217728) ** (-0.5)

    for c in range(2):
        total = land_z[c]
        for i in range(1, 8):
            total = total + land_z[2 * i + c]
        full[me, probe, c] = total * scale

    def plane_copy(n, row, row_probe, member, other_probe):
        place = full.at[row, row_probe]
        return pltpu.make_async_remote_copy(
            src_ref=place, dst_ref=place, send_sem=send_small.at[23 + n], recv_sem=recv_small.at[23 + n],
            device_id=plane_device(member, other_probe), device_id_type=MESH)

    for n, (d, dp) in enumerate(plane):
        copy = plane_copy(n, me, probe, wrap(me + d, 8), probe ^ dp)
        copy.start()
        sent.append(copy)
    for n, (d, dp) in enumerate(plane):
        source = wrap(me - d, 8)
        plane_copy(n, source, probe ^ dp, source, probe ^ dp).wait_recv()

    count = 16384.0

    def mean(value):
        value = jnp.sum(value, axis=(0, 1))
        return jnp.sum(jnp.sum(value, axis=0, keepdims=True), axis=1, keepdims=True) / count

    first, second = full[:, 0], full[:, 1]
    unit = first * lax.rsqrt(mean(first * first) + 1e-06)
    rest = second - mean(unit * second) * unit
    last = rest * lax.rsqrt(mean(rest * rest) + 1e-06)
    by_probe = probe == 0
    for i in range(8):
        at = slice(i * 8, (i + 1) * 8)
        sketch_ref[0, at, :] = jnp.where(by_probe, first[i, 0], first[i, 1])
        sketch_ref[1, at, :] = jnp.where(by_probe, second[i, 0], second[i, 1])
        basis_ref[0, at, :] = jnp.where(by_probe, unit[i, 0], unit[i, 1])
        basis_ref[1, at, :] = jnp.where(by_probe, last[i, 0], last[i, 1])
    for d in range(1, 8):
        xt_copy(d, wrap(me + d, 8), wrap(me + d, 8)).wait_send()
    for copy in sent:
        copy.wait_send()


def whole(tokens_x, cot_t, signs, samples):
    shape = jax.ShapeDtypeStruct((2, 64, 128), F32)
    return pl.pallas_call(
        whole_kernel,
        out_shape=(shape, shape),
        in_specs=[pl.BlockSpec(memory_space=pltpu.HBM)] * 4,
        out_specs=(pl.BlockSpec(memory_space=pltpu.VMEM), pl.BlockSpec(memory_space=pltpu.VMEM)),
        scratch_shapes=[
            pltpu.VMEM((512, 2048), BF16),
            pltpu.VMEM((128, 1024), BF16),
            pltpu.VMEM((64, 768), BF16),
            pltpu.VMEM((512, SIDE), BF16),
            pltpu.VMEM((4, 128, SIDE), F32),
            pltpu.VMEM((3, 64, SIDE), F32),
            pltpu.VMEM((512, SIDE), F32),
            pltpu.VMEM((2, 4096, 128), jnp.int32),
            pltpu.VMEM((224, 512), BF16),
            pltpu.VMEM((224, 512), F32),
            pltpu.VMEM((224, 512), F32),
            pltpu.VMEM((2, 224, 512), F32),
            pltpu.VMEM((512, 512), BF16),
            pltpu.VMEM((512, 512), BF16),
            pltpu.VMEM((SIDE, SIDE), BF16),
            pltpu.VMEM((8, 512, SIDE), F32),
            pltpu.VMEM((8, 512, SIDE), F32),
            pltpu.VMEM((8, 512, SIDE), F32),
            pltpu.VMEM((16384, 128), F32),
            pltpu.VMEM((128, 128), jnp.int32),
            pltpu.VMEM((64, 128), jnp.int32),
            pltpu.SMEM((64, 128), jnp.int32),
            pltpu.VMEM((128, 128), F32),
            pltpu.VMEM((128, 128), F32),
            pltpu.VMEM((8, 8, 128), F32),
            pltpu.VMEM((7, 8, 128), F32),
            pltpu.VMEM((8, 128), F32),
            pltpu.VMEM((16, 8, 128), F32),
            pltpu.VMEM((8, 2, 2, 8, 128), F32),
            pltpu.SemaphoreType.DMA((8,)),
            pltpu.SemaphoreType.DMA((88,)),
            pltpu.SemaphoreType.DMA((88,)),
            pltpu.SemaphoreType.DMA((38,)),
            pltpu.SemaphoreType.DMA((38,)),
        ],
        compiler_params=pltpu.CompilerParams(
            collective_id=0, has_side_effects=True, vmem_limit_bytes=55104 << 10),
        cost_estimate=pl.CostEstimate(flops=8 << 30, bytes_accessed=24 << 20, transcendentals=0),
        name="whole",
    )(tokens_x, cot_t, signs, samples)


def on_device(tokens_x, cotangent, signs, samples):
    sketch, basis = whole(tokens_x, cotangent[0].T, signs.reshape(8192, 128), samples.reshape(128, 128))
    return sketch.reshape(2, 8192), basis.reshape(2, 8192)


def solution(mesh):
    in_specs = (P("tok", None), P("probe", "tok", "param"), P(("param", "tok")), P())
    out_specs = (P(None, "probe"), P(None, "probe"))
    return jax.shard_map(
        on_device, mesh=mesh, in_specs=in_specs, out_specs=out_specs, check_vma=False
    )
```

```python
import functools

import jax
import jax.numpy as jnp
from jax import lax
from jax.experimental import pallas as pl
from jax.experimental.pallas import tpu as pltpu
from jax.sharding import PartitionSpec as P

MESH = pl.DeviceIdType.MESH
RING_X, RING_Z = 4, 8
SIDE = 256
BF16, F32 = jnp.bfloat16, jnp.float32


def position():
    param = lax.axis_index("param")
    z, x, core = param // 8, (param // 2) % 4, param % 2
    return z, x, core, lax.axis_index("tok"), lax.axis_index("probe")


def device(z, x, core, tok, probe):
    return ((z * RING_X + x) * 2 + core, tok, probe)


def wrap(value, size):
    return lax.rem(value + 2 * size, size)


def signed_table(width):
    rows = lax.broadcasted_iota(jnp.int32, (width, width), 0)
    cols = lax.broadcasted_iota(jnp.int32, (width, width), 1)
    bits = rows & cols
    bits = bits ^ (bits >> 4)
    bits = bits ^ (bits >> 2)
    bits = bits ^ (bits >> 1)
    return (1 - 2 * (bits & 1)).astype(F32).astype(BF16)


def split_two(value):
    high = value.astype(BF16)
    return high, (value - high.astype(F32)).astype(BF16)


def butterfly(values):
    values = list(values)
    gap = 1
    while gap < len(values):
        for start in range(0, len(values), 2 * gap):
            for i in range(start, start + gap):
                a, b = values[i], values[i + gap]
                values[i], values[i + gap] = a + b, a - b
        gap *= 2
    return values


FEED = (("n", 1), ("n", 5), ("f", 4), ("f", 2), ("n", "ct"), ("f", 6), ("f", 3), ("n", 7), ("f", 0), ("f", 7))
ORDER = (
    "z40 x10 z50 x20", "z41 z60 p00 z51", "x11 p10 x30 z42", "p20 z61 x21 p30", "x00 z52 z43 x12",
    "c00 z62 z53 x31", "x22 c10 m10 m20", "z44 m40 z63 x01", "z54 m50 y70 m70", "x32 m30 z64 m60",
    "q20 x02 m00 q10", "q30 q00",
)


def whole_kernel(
    x_ref, ct_ref, signs_ref, samples_ref, sketch_ref, basis_ref,
    xh, xfb, zfb, yfb, xf, zf, yf, sg, ct_raw, ct_send, ct_mate, ct_land, ct_own, ct_other, table,
    xo, base, sign_t, grid, samples, index_v, index_s,
    rows, rows_b, mine, land_xt, red, land_z, full,
    local_sem, send_sem, recv_sem, send_small, recv_small,
):
    z, x, core, tok, probe = position()
    half = 4096
    near = device(z, x, core, 1 - tok, probe)
    far = device(z, x, core, 1 - tok, 1 - probe)
    right_x = device(z, wrap(x + 1, RING_X), core, tok, probe)
    left_x = device(z, wrap(x - 1, RING_X), core, tok, probe)
    right_z = device(wrap(z + 1, RING_Z), x, core, tok, probe)
    left_z = device(wrap(z - 1, RING_Z), x, core, tok, probe)
    sibling = device(z, x, 1 - core, tok, probe)
    me = x * 2 + tok

    def xt_device(member):
        return device(z, member // 2, core, member % 2, probe)

    def column_device(other_z, other_core):
        return device(other_z, x, other_core, tok, probe)

    def plane_device(member, other_probe):
        return device(z, member // 2, core, member % 2, other_probe)

    column = [(dz, dc) for dz in (4, 3, 5, 2, 6, 1, 7, 0) for dc in (1, 0)][:-1]
    plane = [(d, dp) for d in (4, 5, 3, 2, 6, 7, 1, 0) for dp in (1, 0)][:-1]

    mine_at = pl.multiple_of(tok * half + core * 2048, 128)
    theirs = pl.multiple_of((1 - tok) * half + core * 2048, 128)
    loads = [
        pltpu.make_async_copy(
            x_ref.at[pl.ds(pl.multiple_of(64 * z, 64), 64), pl.ds(theirs + 1024, 768)], zfb, local_sem.at[0]),
        pltpu.make_async_copy(
            x_ref.at[pl.ds(pl.multiple_of(128 * x, 128), 128), pl.ds(theirs, 1024)], xfb, local_sem.at[1]),
        pltpu.make_async_copy(ct_ref, ct_raw, local_sem.at[2]),
        pltpu.make_async_copy(x_ref.at[:, pl.ds(theirs + 1792, SIDE)], yfb, local_sem.at[3]),
        pltpu.make_async_copy(samples_ref, samples, local_sem.at[4]),
        pltpu.make_async_copy(x_ref.at[:, pl.ds(mine_at, 2048)], xh, local_sem.at[5]),
        pltpu.make_async_copy(
            signs_ref.at[pl.ds(pl.multiple_of(core * half, half), half)], sg.at[core], local_sem.at[6]),
    ]
    for load in loads[:2]:
        load.start()

    barrier = pltpu.get_barrier_semaphore()
    partners = [plane_device(wrap(me + d, 8), probe ^ dp) for d, dp in plane]
    partners += [column_device(wrap(z + dz, 8), core ^ dc) for dz, dc in column]
    for partner in partners:
        pl.semaphore_signal(barrier, inc=1, device_id=partner, device_id_type=MESH)
    for load in loads[2:]:
        load.start()

    numbers = {}
    sent = []

    def number(name):
        return numbers.setdefault(name, len(numbers))

    def send(name, src, dst, target):
        n = number(name)
        copy = pltpu.make_async_remote_copy(
            src_ref=src, dst_ref=dst, send_sem=send_sem.at[n], recv_sem=recv_sem.at[n],
            device_id=target, device_id_type=MESH)
        copy.start()
        sent.append(copy)
        return copy

    def arrived(name, dst, source):
        n = number(name)
        pltpu.make_async_remote_copy(
            src_ref=dst, dst_ref=dst, send_sem=send_sem.at[n], recv_sem=recv_sem.at[n],
            device_id=source, device_id_type=MESH).wait_recv()

    def xs(k, i):
        return xo.at[k, pl.ds(pl.multiple_of(128 * wrap(i, RING_X), 128), 128)]

    def xs_part(k, i, part):
        return xo.at[k, pl.ds(pl.multiple_of(128 * wrap(i, RING_X) + part, 64), 64)]

    def zs(k, i):
        return xo.at[k, pl.ds(pl.multiple_of(64 * wrap(i, RING_Z), 64), 64)]

    loads[0].wait()
    for j in range(3):
        zf[j] = zfb[:, j * SIDE:(j + 1) * SIDE].astype(F32)
    loads[1].wait()
    for j in range(4):
        xf[j] = xfb[:, j * SIDE:(j + 1) * SIDE].astype(F32)
    pl.semaphore_wait(barrier, len(partners))

    route = {}
    split = {k for _, k in FEED if k != 7 and sum(entry[1] == k for entry in FEED) == 2}
    for side, k in FEED:
        target = near if side == "n" else far
        if k == "ct":
            loads[2].wait()
            ct_send[...] = ct_raw[...].astype(F32)
            send("ct", ct_send, ct_land.at[core], target)
        elif k == 7:
            if side == "n":
                loads[3].wait()
                yf[...] = yfb[...].astype(F32)
            part = pl.ds(0 if side == "n" else 256, 256)
            send(("feed", 7, side), yf.at[part], xo.at[7, part], target)
        else:
            route[k] = target
            if k in split:
                part = 0 if side == "n" else 64
                send(("feed", k, side), xf.at[k, pl.ds(part, 64)], xs_part(k, x, part), target)
            elif k < 4:
                send(("feed", k), xf.at[k], xs(k, x), target)
            else:
                send(("feed", k), zf.at[k - 4], zs(k, z), target)

    send("mate", ct_send, ct_mate, sibling)
    send("signs", signs_ref.at[pl.ds(pl.multiple_of((1 - core) * half, half), half)], sg.at[core], sibling)
    table[...] = signed_table(SIDE)
    ct_own[...] = jnp.zeros_like(ct_own)
    ct_other[...] = jnp.zeros_like(ct_other)
    own_rows = pl.ds(pl.multiple_of(core * SIDE, SIDE), 224)
    mate_rows = pl.ds(pl.multiple_of((1 - core) * SIDE, SIDE), 224)
    ct_own[own_rows, :] = ct_raw[...]
    loads[4].wait()
    m = samples[pl.ds(pl.multiple_of(core * 64, 64), 64), :]
    index_v[...] = ((m >> 16 & 15) << 10) | ((m >> 21 & 1) << 9) | ((m >> 15 & 1) << 8) | (m & 255)
    to_scalar = pltpu.make_async_copy(index_v, index_s, local_sem.at[7])
    to_scalar.start()
    loads[5].wait()
    loads[6].wait()
    arrived("mate", ct_mate, sibling)
    ct_own[mate_rows, :] = ct_mate[...].astype(BF16)
    arrived("signs", sg.at[1 - core], sibling)

    def prepare(part):
        def body(i, carry):
            k = 2 * part + i
            product = jnp.dot(
                ct_own[...], xh[:, pl.ds(pl.multiple_of(SIDE * k, SIDE), SIDE)], preferred_element_type=F32)
            for b in range(2):
                even = sg[b, pl.ds(pl.multiple_of(512 * k, 512), SIDE, stride=2), :]
                odd = sg[b, pl.ds(pl.multiple_of(512 * k, 512) + 1, SIDE, stride=2), :]
                turned = jnp.concatenate([even.astype(F32).T, odd.astype(F32).T], axis=0)
                rows_b = slice(b * SIDE, (b + 1) * SIDE)
                sign_t[k, rows_b, :] = turned
                base[k, rows_b, :] = turned * product[rows_b]
            return carry

        lax.fori_loop(0, 2, body, 0)

    def place_of(g, sel):
        return grid.at[pl.ds(pl.multiple_of(g * 1024 + sel * 512, 512), 512)]

    sent_grid = {}

    def process(k):
        h = table[...]
        product = jnp.dot(ct_other[...], xo[k].astype(BF16), preferred_element_type=F32)
        value = base[k] + sign_t[k] * product
        at = (core * 8 + k) * 1024
        for sel in range(2):
            both = value[:SIDE] + value[SIDE:] if sel == 0 else value[:SIDE] - value[SIDE:]
            high, low = split_two(both)
            mixed = jnp.dot(h, high, preferred_element_type=F32) + jnp.dot(h, low, preferred_element_type=F32)
            high, low = split_two(mixed)
            mixed = jnp.dot(high, h, preferred_element_type=F32) + jnp.dot(low, h, preferred_element_type=F32)
            for part in range(2):
                first_row = pl.multiple_of(at + (sel * 2 + part) * SIDE, SIDE)
                grid[pl.ds(first_row, SIDE), :] = mixed[:, part * 128:(part + 1) * 128]
            place = place_of(core * 8 + k, sel)
            sent_grid[k, sel] = send(("grid", k, sel), place, place, sibling)

    def quad(q):
        for k in (2 * q, 2 * q + 1):
            for sel in range(2):
                arrived(("grid", k, sel), place_of((1 - core) * 8 + k, sel), sibling)
                sent_grid[k, sel].wait_send()
                sent[:] = [copy for copy in sent if copy is not sent_grid[k, sel]]

        def body(i, carry):
            rows_of = [
                [pl.ds(pl.multiple_of(g * 1024 + i * 64 + r, 16), 16) for g in (2 * q, 2 * q + 1, 8 + 2 * q, 9 + 2 * q)]
                for r in range(0, 64, 16)]
            values = [butterfly([grid[place, :] for place in places]) for places in rows_of]
            for places, results in zip(rows_of, values):
                for place, result in zip(places, results):
                    grid[place, :] = result
            return carry

        lax.fori_loop(0, 16, body, 0, unroll=4)

    def take_ct(step):
        if step == 0:
            arrived("ct", ct_land.at[core], near)
            send("ct2", ct_land.at[core], ct_land.at[core], sibling)
            ct_other[own_rows, :] = ct_land[core].astype(BF16)
        else:
            arrived("ct2", ct_land.at[1 - core], sibling)
            ct_other[mate_rows, :] = ct_land[1 - core].astype(BF16)

    def hop_x(k, d):
        if d == 0:
            if k in split:
                arrived(("feed", k, "n"), xs_part(k, x, 0), near)
                arrived(("feed", k, "f"), xs_part(k, x, 64), far)
            else:
                arrived(("feed", k), xs(k, x), route[k])
            send(("xr", k), xs(k, x), xs(k, x), right_x)
            send(("xl", k), xs(k, x), xs(k, x), left_x)
        elif d == 1:
            arrived(("xr", k), xs(k, x - 1), left_x)
            if k % 2 == 0:
                send(("xe", k), xs(k, x - 1), xs(k, x - 1), right_x)
            arrived(("xl", k), xs(k, x + 1), right_x)
            if k % 2 == 1:
                send(("xe", k), xs(k, x + 1), xs(k, x + 1), left_x)
        else:
            arrived(("xe", k), xs(k, x + 2), left_x if k % 2 == 0 else right_x)

    def hop_z(k, d):
        if d == 0:
            arrived(("feed", k), zs(k, z), route[k])
            send(("zr", k, 1), zs(k, z), zs(k, z), right_z)
            send(("zl", k, 1), zs(k, z), zs(k, z), left_z)
        elif d < 4:
            arrived(("zr", k, d), zs(k, z - d), left_z)
            if d < 3 or k % 2 == 0:
                send(("zr", k, d + 1), zs(k, z - d), zs(k, z - d), right_z)
            arrived(("zl", k, d), zs(k, z + d), right_z)
            if d < 3 or k % 2 == 1:
                send(("zl", k, d + 1), zs(k, z + d), zs(k, z + d), left_z)
        else:
            if k % 2 == 0:
                arrived(("zr", k, 4), zs(k, z - 4), left_z)
            else:
                arrived(("zl", k, 4), zs(k, z + 4), right_z)

    def hop_y(k):
        arrived(("feed", k, "n"), xo.at[k, pl.ds(0, 256)], near)
        arrived(("feed", k, "f"), xo.at[k, pl.ds(256, 256)], far)

    for step in " ".join(ORDER).split():
        kind, k, d = step[0], int(step[1]), int(step[2])
        if kind == "x":
            hop_x(k, d)
        elif kind == "z":
            hop_z(k, d)
        elif kind == "y":
            hop_y(k)
        elif kind == "c":
            take_ct(k)
        elif kind == "p":
            prepare(k)
        elif kind == "m":
            process(k)
        else:
            quad(k)

    def last(i, carry):
        at = (i // 32) * 8192 + (i // 16 % 2) * 1024 + (i % 16) * 64
        rows_of = [
            [pl.ds(pl.multiple_of(at + q * 2048 + r, 16), 16) for q in range(4)] for r in range(0, 64, 16)]
        values = [butterfly([grid[place, :] for place in places]) for places in rows_of]
        for places, results in zip(rows_of, values):
            for place, result in zip(places, results):
                grid[place, :] = result
        return carry

    lax.fori_loop(0, 64, last, 0, unroll=4)
    to_scalar.wait()
    code = tok | (x << 2) | (z << 4)
    lanes = lax.broadcasted_iota(jnp.int32, (128, 128), 0)

    def place_in(n):
        return wrap(me + 1 + n // 8, 8), n % 8

    def gather(n, to):
        piece, b = place_in(n)
        for r in range(0, 128, 8):
            to[r:r + 8, :] = jnp.concatenate(
                [grid[pl.ds(index_s[piece * 8 + b, r + k], 1), :] for k in range(8)], axis=0)

    def pick(n, got):
        piece, b = place_in(n)
        m = samples[pl.ds(core * 64 + piece * 8 + b, 1), :]
        picked = jnp.where(lanes == ((m >> 8) & 127), got[...].T, 0.0)
        value = jnp.sum(picked, axis=0, keepdims=True)
        odd = (m >> 20) & code
        odd = odd ^ (odd >> 4)
        odd = odd ^ (odd >> 2)
        odd = odd ^ (odd >> 1)
        mine[piece, pl.ds(b, 1), :] = jnp.where((odd & 1) == 1, -value, value)

    def xt_copy(d, piece, member):
        return pltpu.make_async_remote_copy(
            src_ref=mine.at[piece], dst_ref=land_xt.at[d - 1], send_sem=send_small.at[d - 1],
            recv_sem=recv_small.at[d - 1], device_id=xt_device(member), device_id_type=MESH)

    def gather_step(i, carry):
        gather(2 * i + 1, rows_b)
        pick(2 * i, rows)
        gather(jnp.minimum(2 * i + 2, 63), rows)
        pick(2 * i + 1, rows_b)

        @pl.when(jnp.logical_and(i % 4 == 3, i < 28))
        def _():
            d = i // 4 + 1
            piece = wrap(me + d, 8)
            xt_copy(d, piece, piece).start()

        return carry

    gather(0, rows)
    lax.fori_loop(0, 32, gather_step, 0)
    total = mine[me]
    for d in range(1, 8):
        xt_copy(d, wrap(me + d, 8), wrap(me - d, 8)).wait_recv()
        total = total + land_xt[d - 1]
    red[...] = total

    def column_copy(source, target):
        return pltpu.make_async_remote_copy(
            src_ref=red, dst_ref=land_z.at[source], send_sem=send_small.at[7 + target],
            recv_sem=recv_small.at[7 + source], device_id=column_device(target // 2, target % 2), device_id_type=MESH)

    here = z * 2 + core
    for dz, dc in column:
        copy = column_copy(here, wrap(z + dz, 8) * 2 + (core ^ dc))
        copy.start()
        sent.append(copy)
    land_z[here] = total
    for dz, dc in column:
        column_copy(wrap(z - dz, 8) * 2 + (core ^ dc), here).wait_recv()
    scale = float(1024 * 134217728) ** (-0.5)

    for c in range(2):
        total = land_z[c]
        for i in range(1, 8):
            total = total + land_z[2 * i + c]
        full[me, probe, c] = total * scale

    def plane_copy(n, row, row_probe, member, other_probe):
        place = full.at[row, row_probe]
        return pltpu.make_async_remote_copy(
            src_ref=place, dst_ref=place, send_sem=send_small.at[23 + n], recv_sem=recv_small.at[23 + n],
            device_id=plane_device(member, other_probe), device_id_type=MESH)

    for n, (d, dp) in enumerate(plane):
        copy = plane_copy(n, me, probe, wrap(me + d, 8), probe ^ dp)
        copy.start()
        sent.append(copy)
    for n, (d, dp) in enumerate(plane):
        source = wrap(me - d, 8)
        plane_copy(n, source, probe ^ dp, source, probe ^ dp).wait_recv()

    count = 16384.0

    def mean(value):
        value = jnp.sum(value, axis=(0, 1))
        return jnp.sum(jnp.sum(value, axis=0, keepdims=True), axis=1, keepdims=True) / count

    first, second = full[:, 0], full[:, 1]
    unit = first * lax.rsqrt(mean(first * first) + 1e-06)
    rest = second - mean(unit * second) * unit
    last = rest * lax.rsqrt(mean(rest * rest) + 1e-06)
    by_probe = probe == 0
    for i in range(8):
        at = slice(i * 8, (i + 1) * 8)
        sketch_ref[0, at, :] = jnp.where(by_probe, first[i, 0], first[i, 1])
        sketch_ref[1, at, :] = jnp.where(by_probe, second[i, 0], second[i, 1])
        basis_ref[0, at, :] = jnp.where(by_probe, unit[i, 0], unit[i, 1])
        basis_ref[1, at, :] = jnp.where(by_probe, last[i, 0], last[i, 1])
    for d in range(1, 8):
        xt_copy(d, wrap(me + d, 8), wrap(me + d, 8)).wait_send()
    for copy in sent:
        copy.wait_send()


def whole(tokens_x, cot_t, signs, samples):
    shape = jax.ShapeDtypeStruct((2, 64, 128), F32)
    return pl.pallas_call(
        whole_kernel,
        out_shape=(shape, shape),
        in_specs=[pl.BlockSpec(memory_space=pltpu.HBM)] * 4,
        out_specs=(pl.BlockSpec(memory_space=pltpu.VMEM), pl.BlockSpec(memory_space=pltpu.VMEM)),
        scratch_shapes=[
            pltpu.VMEM((512, 2048), BF16),
            pltpu.VMEM((128, 1024), BF16),
            pltpu.VMEM((64, 768), BF16),
            pltpu.VMEM((512, SIDE), BF16),
            pltpu.VMEM((4, 128, SIDE), F32),
            pltpu.VMEM((3, 64, SIDE), F32),
            pltpu.VMEM((512, SIDE), F32),
            pltpu.VMEM((2, 4096, 128), jnp.int32),
            pltpu.VMEM((224, 512), BF16),
            pltpu.VMEM((224, 512), F32),
            pltpu.VMEM((224, 512), F32),
            pltpu.VMEM((2, 224, 512), F32),
            pltpu.VMEM((512, 512), BF16),
            pltpu.VMEM((512, 512), BF16),
            pltpu.VMEM((SIDE, SIDE), BF16),
            pltpu.VMEM((8, 512, SIDE), F32),
            pltpu.VMEM((8, 512, SIDE), F32),
            pltpu.VMEM((8, 512, SIDE), F32),
            pltpu.VMEM((16384, 128), F32),
            pltpu.VMEM((128, 128), jnp.int32),
            pltpu.VMEM((64, 128), jnp.int32),
            pltpu.SMEM((64, 128), jnp.int32),
            pltpu.VMEM((128, 128), F32),
            pltpu.VMEM((128, 128), F32),
            pltpu.VMEM((8, 8, 128), F32),
            pltpu.VMEM((7, 8, 128), F32),
            pltpu.VMEM((8, 128), F32),
            pltpu.VMEM((16, 8, 128), F32),
            pltpu.VMEM((8, 2, 2, 8, 128), F32),
            pltpu.SemaphoreType.DMA((8,)),
            pltpu.SemaphoreType.DMA((88,)),
            pltpu.SemaphoreType.DMA((88,)),
            pltpu.SemaphoreType.DMA((38,)),
            pltpu.SemaphoreType.DMA((38,)),
        ],
        compiler_params=pltpu.CompilerParams(
            collective_id=0, has_side_effects=True, vmem_limit_bytes=55104 << 10),
        cost_estimate=pl.CostEstimate(flops=8 << 30, bytes_accessed=24 << 20, transcendentals=0),
        name="whole",
    )(tokens_x, cot_t, signs, samples)


def on_device(tokens_x, cotangent, signs, samples):
    sketch, basis = whole(tokens_x, cotangent[0].T, signs.reshape(8192, 128), samples.reshape(128, 128))
    return sketch.reshape(2, 8192), basis.reshape(2, 8192)


def solution(mesh):
    in_specs = (P("tok", None), P("probe", "tok", "param"), P(("param", "tok")), P())
    out_specs = (P(None, "probe"), P(None, "probe"))
    return jax.shard_map(
        on_device, mesh=mesh, in_specs=in_specs, out_specs=out_specs, check_vma=False
    )
```
